128 devices in a mesh: lon: 8 (over x, z_lo), lat: 16 (over y, z_hi, core).
Axes of the slice: x: 4, y: 4, z: 4 (z_hi: 2, z_lo: 2; z = z_hi * 2 + z_lo), core: 2. Of those that a mesh axis runs over, the one named last changes fastest.
Arguments:
- prior_state: float32 [64, 64, 64, 256], P('lon', 'lat'), may hold values from -3 to 3
- courant: float32 [64, 64], P('lon', 'lat'), may hold values from 0.2 to 0.8
- cell_survival_rate: float32 [64], replicated, may hold values from 0.8 to 1
- geometry: float32 [16, 64, 128], replicated, may hold values from 0.005 to 0.05
- entry_tile: int32 [8, 16, 64], P('lon', 'lat'), may hold values from 0 to 31, as said below
- entry_column: int32 [8, 16, 64], P('lon', 'lat'), may hold values from 0 to 31
- entry_segment: int32 [8, 16, 64], P('lon', 'lat'), may hold values from 0 to 15
- entry_counts: int32 [8, 16], P('lon', 'lat'), may hold values from 1 to 64, as said below
- observed: float32 [4, 8, 32, 128], P(None, 'lon', 'lat'), may hold values from -6 to 6
- obs_weight: float32 [4, 8, 32, 128], P(None, 'lon', 'lat'), may hold values from 0.02 to 0.08
Outputs:
- start_state: float32 [64, 64, 64, 256], P('lon', 'lat')
- end_state: float32 [64, 64, 64, 256], P('lon', 'lat')
The draws below stay inside these ranges and needn't reach their ends.
Inputs may be any that keep to these rules, and one draw needn't show every extreme that they name: The owning band entry_tile // 2 of every entry is the device's own latitude band or one beside it. Entries at positions at or beyond the device's count are padding and are ignored. `entry_counts`: some device holds exactly 64 live entries.
All inputs are finite; a program needn't handle non-finite values.
Results may differ from the reference program's by a relative error of at most 0.0003.
Values sent between devices are 32-bit elements; how exact they have to be, the bound alone decides.
A program may use at most 128 MiB of HBM per device.

```python
import math
import jax
import jax.numpy as jnp
from jax import lax

ALT = 64
RAYS = 128
SEG = 16
STEPS = 4
CLON = 8
CLAT = 4
E_DEV = 64
TILE_DEV = 2
WIDE = 256
NLON = 64
NLAT = 64
TILES_SEC = 32
N_LON = 8
N_LAT = 16


def draw_entry_tile(key, part):
    key_one, key_two = jax.random.split(key, 2)
    shape_all = (N_LON, N_LAT, E_DEV)
    band_ids = jnp.arange(N_LAT, dtype=jnp.int32)[None, :, None]
    offset_draw = jax.random.randint(key_one, shape_all, -1, 2)
    target = jnp.clip(band_ids + offset_draw, 0, N_LAT - 1)
    tiles_all = target * TILE_DEV + jax.random.randint(key_two, shape_all, 0, TILE_DEV)
    tiles_all = tiles_all.at[0, 0, 0].set(0)
    tiles_all = tiles_all.at[0, N_LAT - 1, 0].set(N_LAT * TILE_DEV - 1)
    return tiles_all.astype(jnp.int32)


def draw_entry_counts(key, part):
    key_one, key_two, key_three = jax.random.split(key, 3)
    shape_all = (N_LON, N_LAT)
    level_draw = jax.random.randint(key_one, shape_all, 0, 4)
    full_count = jnp.right_shift(jnp.full(shape_all, E_DEV, dtype=jnp.int32), level_draw)
    jitter = jax.random.randint(key_two, shape_all, 0, E_DEV // 8 + 1)
    counts = jnp.maximum(full_count - jitter, 1)
    chosen = jax.random.randint(key_three, (), 0, N_LON * N_LAT)
    flat_ids = jnp.arange(N_LON * N_LAT, dtype=jnp.int32).reshape(shape_all)
    counts = jnp.where(flat_ids == chosen, E_DEV, counts)
    return counts.astype(jnp.int32)


def place_ends(array, own_key, low, top_value):
    longest = array.shape.index(max(array.shape))
    spots = []
    for shift in (0, 1):
        where = [jax.random.randint(jax.random.fold_in(own_key, axis), (), 0, length) for axis, length in enumerate(array.shape)]
        where[longest] = (where[longest] + shift) % array.shape[longest]
        spots.append(tuple(where))
    return array.at[spots[0]].set(low).at[spots[1]].set(top_value)


def steps_of(stream_key, shape, cuts, low, high):
    gain = 1.0
    for dim, parts in cuts:
        steps = jax.random.uniform(jax.random.fold_in(jax.random.fold_in(stream_key, 6), dim), (parts,), jnp.float32, low / len(cuts), high / len(cuts))
        gain = gain * jnp.repeat(jnp.exp(steps), shape[dim] // parts).reshape((-1,) + (1,) * (len(shape) - 1 - dim))
    return gain


def normal_values(stream_key, dims, deviation, most, cuts=(), kind=jnp.bfloat16):
    level = steps_of(stream_key, dims, cuts, -0.22, 0.18) if cuts else 1.0
    result = jax.random.normal(stream_key, dims, jnp.float32) * deviation * level
    return jnp.minimum(jnp.maximum(result, -most), most).astype(kind)


def setup_inputs(seed: int = 0) -> dict:
    streams_of = jax.random.split(jax.random.key(seed), 11)
    return {
        "prior_state": normal_values(streams_of[0], (NLON, NLAT, ALT, WIDE), 0.5, 3.0, ((0, 8), (1, 16)), jnp.float32),
        "courant": jnp.clip(0.2 + 0.6 * jax.random.uniform(streams_of[1], (NLON, NLAT), jnp.float32) ** steps_of(streams_of[1], (NLON, NLAT), ((0, 8), (1, 16)), -0.2, 0.2), 0.2, 0.8),
        "cell_survival_rate": jnp.clip(jax.random.uniform(streams_of[2], (ALT,), jnp.float32, 0.8, 1.0), 0.8, 1.0),
        "geometry": jnp.clip(jnp.exp(jax.random.uniform(streams_of[3], (SEG, ALT, RAYS), jnp.float32, math.log(0.005), math.log(0.05))), 0.005, 0.05),
        "entry_tile": draw_entry_tile(jax.random.fold_in(streams_of[10], 71), 0),
        "entry_column": place_ends(jax.random.randint(streams_of[5], (N_LON, N_LAT, E_DEV), 0, CLON * CLAT), jax.random.fold_in(streams_of[5], 1), 0, (CLON * CLAT) - 1).astype(jnp.int32),
        "entry_segment": place_ends(jax.random.randint(streams_of[6], (N_LON, N_LAT, E_DEV), 0, SEG), jax.random.fold_in(streams_of[6], 1), 0, SEG - 1).astype(jnp.int32),
        "entry_counts": draw_entry_counts(jax.random.fold_in(streams_of[10], 71), 0),
        "observed": normal_values(streams_of[8], (STEPS, N_LON, TILES_SEC, RAYS), 1.0, 6.0, ((1, 8), (2, 16)), jnp.float32),
        "obs_weight": jnp.clip(jnp.exp(math.log(0.08) - 1.3862944 * jax.random.uniform(streams_of[9], (STEPS, N_LON, TILES_SEC, RAYS), jnp.float32) ** steps_of(streams_of[9], (STEPS, N_LON, TILES_SEC, RAYS), ((1, 8), (2, 16)), -0.2, 0.2)), 0.02, 0.08),
    }


diffusion = 0.08
highest = lax.Precision.HIGHEST

def predicted_state(current_state, courant, cell_survival_rate):
    behind = jnp.roll(current_state, 1, axis=0)
    padded = jnp.pad(current_state, ((0, 0), (1, 1), (0, 0), (0, 0)))
    spread = padded[:, 2:] + padded[:, :-2] - 2.0 * current_state
    moved = current_state - courant[:, :, None, None] * (current_state - behind) + diffusion * spread
    return cell_survival_rate[None, None, :, None] * moved

def state_mapping(gram_total):
    width_all = gram_total.shape[0]
    identity = jnp.eye(width_all - 1, dtype=jnp.float32)
    chol_lower = jnp.linalg.cholesky(identity + gram_total[1:, 1:])
    inverse = lax.linalg.triangular_solve(chol_lower, identity, left_side=True, lower=True)
    inner = jnp.dot(inverse, gram_total[1:, 0], precision=highest)
    weights = jnp.dot(inner, inverse, precision=highest)
    first_row = (jnp.arange(width_all) == 0).astype(jnp.float32)[None, :]
    lower_rows = jnp.concatenate([weights[:, None], inverse.T], axis=1)
    return jnp.concatenate([first_row, lower_rows], axis=0)

def pick_columns(band_block, column_ids):
    return band_block[column_ids]

def reference(prior_state, courant, cell_survival_rate, geometry, entry_tile, entry_column, entry_segment, entry_counts, observed, obs_weight):
    current_state = prior_state
    lagged = prior_state
    slot_index = jnp.arange(E_DEV, dtype=jnp.int32)
    tile_index = jnp.arange(TILES_SEC, dtype=jnp.int32)

    def sector_sums(pieces):
        sector_state, tiles_here, columns_here, segments_here, counts_here = pieces
        per_band_rows = sector_state.reshape(CLON, N_LAT, CLAT, ALT, WIDE).transpose(1, 0, 2, 3, 4).reshape(N_LAT, CLON * CLAT, ALT, WIDE)
        columns = jax.vmap(pick_columns)(per_band_rows, columns_here)
        paths = geometry[segments_here]
        block_list = jnp.einsum('bear,beak->berk', paths, columns, precision=highest)
        live_slot = slot_index[None, :] < counts_here[:, None]
        select = ((tiles_here[:, None, :] == tile_index[None, :, None]) & live_slot[:, None, :]).astype(jnp.float32)
        return jnp.einsum('bte,berk->trk', select, block_list, precision=highest)
    for step_index in range(STEPS):
        current_state = predicted_state(current_state, courant, cell_survival_rate)
        by_sector = current_state.reshape(N_LON, CLON, NLAT, ALT, WIDE)
        projected = lax.map(sector_sums, (by_sector, entry_tile, entry_column, entry_segment, entry_counts))
        weight_now = obs_weight[step_index]
        innovation = (observed[step_index] - projected[..., 0]) * weight_now
        scaled = projected[..., 1:] * weight_now[..., None]
        mixed_rows = jnp.concatenate([innovation[..., None], scaled], axis=-1).reshape(-1, WIDE)
        gram_total = lax.dot_general(mixed_rows, mixed_rows, (((0,), (0,)), ((), ())), precision=highest)
        update = state_mapping(gram_total)
        current_state = jnp.dot(current_state.reshape(-1, WIDE), update, precision=highest).reshape(current_state.shape)
        lagged = jnp.dot(lagged.reshape(-1, WIDE), update, precision=highest).reshape(lagged.shape)
    return (lagged, current_state)
```

```python
import jax
import jax.numpy as jnp
from jax import lax
from jax.sharding import PartitionSpec as P

STEPS = 4


diffusion = 0.08
highest = lax.Precision.HIGHEST


def from_behind(x, axis, by):
    devices = lax.axis_size(axis)
    return lax.ppermute(x, axis, [(i, (i + by) % devices) for i in range(devices)])


def extended(cells, sides, width):
    for axis, dim in sides:
        count = lax.axis_size(axis)
        ends = count - 1
        head = lax.slice_in_dim(cells, 0, width, axis=dim)
        tail = lax.slice_in_dim(cells, cells.shape[dim] - width, cells.shape[dim], axis=dim)
        cells = jnp.concatenate(
            [
                lax.ppermute(tail, axis, [(i, (i + 1) % count) for i in range(ends)]),
                cells,
                lax.ppermute(head, axis, [((i + 1) % count, i) for i in range(ends)]),
            ],
            axis=dim,
        )
    return cells


def predicted_state(current_state, courant_number_grid, decay_grid):
    upwind_plane = from_behind(current_state[-1:], "lon", 1)
    behind = jnp.concatenate([upwind_plane, current_state[:-1]], axis=0)
    padded = extended(current_state, (("lat", 1),), 1)
    spread = padded[:, 2:] + padded[:, :-2] - 2.0 * current_state
    moved = current_state - courant_number_grid * (current_state - behind) + diffusion * spread
    return decay_grid * moved


def state_mapping(gram_total):
    width_all = gram_total.shape[0]
    identity = jnp.eye(width_all - 1, dtype=jnp.float32)
    chol_lower = jnp.linalg.cholesky(identity + gram_total[1:, 1:])
    inverse = lax.linalg.triangular_solve(chol_lower, identity, left_side=True, lower=True)
    inner = jnp.dot(inverse, gram_total[1:, 0], precision=highest)
    weights = jnp.dot(inner, inverse, precision=highest)
    first_row = (jnp.arange(width_all) == 0).astype(jnp.float32)[None, :]
    lower_rows = jnp.concatenate([weights[:, None], inverse.T], axis=1)
    return jnp.concatenate([first_row, lower_rows], axis=0)


def shards(
    prior_state,
    courant,
    cell_survival_rate,
    geometry,
    entry_tile,
    entry_column,
    entry_segment,
    entry_counts,
    observed,
    obs_weight,
):
    lon_cells, lat_cells, alt_cells, width_all = prior_state.shape
    tile_dev = observed.shape[2]
    ray_count = observed.shape[3]
    tiles_here = entry_tile[0, 0]
    columns_here = entry_column[0, 0]
    slot_total = tiles_here.shape[0]
    slot_index = jnp.arange(slot_total, dtype=jnp.int32)
    live_slot = slot_index < entry_counts[0, 0]
    paths = geometry[entry_segment[0, 0]]
    courant_number_grid = courant[:, :, None, None]
    decay_grid = cell_survival_rate[None, None, :, None]
    my_band = lax.axis_index("lat")
    near_ids = (my_band - 1) * tile_dev + jnp.arange(3 * tile_dev, dtype=jnp.int32)
    near_select = ((tiles_here[None, :] == near_ids[:, None]) & live_slot[None, :]).astype(
        jnp.float32
    )
    current_state = prior_state
    gram_local = jnp.zeros((width_all, width_all), jnp.float32)
    for step_index in range(STEPS):
        current_state = predicted_state(current_state, courant_number_grid, decay_grid)
        columns = current_state.reshape(lon_cells * lat_cells, alt_cells, width_all)[columns_here]
        block_list = jnp.einsum("ear,eak->erk", paths, columns, precision=highest).reshape(
            slot_total, ray_count * width_all
        )
        near_sums = jnp.dot(near_select, block_list, precision=highest).reshape(
            3, tile_dev * ray_count, width_all
        )
        padded = extended(near_sums, (("lat", 0),), 1)
        own_sums = padded[0] + padded[2] + padded[4]
        projected = own_sums.reshape(tile_dev, ray_count, width_all)
        weight_now = obs_weight[step_index, 0]
        innovation = (observed[step_index, 0] - projected[:, :, 0]) * weight_now
        scaled = projected[:, :, 1:] * weight_now[:, :, None]
        mixed_rows = jnp.concatenate([innovation[:, :, None], scaled], axis=2).reshape(
            -1, width_all
        )
        gram_local = gram_local + lax.dot_general(
            mixed_rows, mixed_rows, (((0,), (0,)), ((), ())), precision=highest
        )
    gram_total = lax.psum(gram_local, ("lon", "lat"))
    update = state_mapping(gram_total)
    end_state = jnp.dot(
        current_state.reshape(-1, width_all), update, precision=highest
    ).reshape(current_state.shape)
    start_state = jnp.dot(
        prior_state.reshape(-1, width_all), update, precision=highest
    ).reshape(prior_state.shape)
    return (start_state, end_state)


def solution(mesh):
    placed = (
        P("lon", "lat", None, None),
        P("lon", "lat"),
        P(),
        P(),
        P("lon", "lat", None),
        P("lon", "lat", None),
        P("lon", "lat", None),
        P("lon", "lat"),
        P(None, "lon", "lat", None),
        P(None, "lon", "lat", None),
    )
    return jax.shard_map(
        shards,
        mesh=mesh,
        in_specs=placed,
        out_specs=(P("lon", "lat", None, None), P("lon", "lat", None, None)),
        check_vma=False,
    )
```

```python
import functools
import jax
import jax.numpy as jnp
from jax import lax
from jax.experimental import pallas as pl
from jax.experimental.pallas import tpu as pltpu
from jax.sharding import PartitionSpec as P

STEPS = 4
diffusion = 0.08
highest = lax.Precision.HIGHEST
MESH = pl.DeviceIdType.MESH
F32 = jnp.float32
BF16 = jnp.bfloat16

LON, LAT, ALT, WIDE = 8, 4, 64, 256
RAYS, SEG, TILES = 128, 16, 2
ROWS = TILES * RAYS
NEAR = 3 * TILES
PAIRS = LON * LAT // 2
HALF = 128
PACKED = WIDE + HALF


def state_mapping(gram_total):
    width_all = gram_total.shape[0]
    identity = jnp.eye(width_all - 1, dtype=jnp.float32)
    chol_lower = jnp.linalg.cholesky(identity + gram_total[1:, 1:])
    inverse = lax.linalg.triangular_solve(chol_lower, identity, left_side=True, lower=True)
    inner = jnp.dot(inverse, gram_total[1:, 0], precision=highest)
    weights = jnp.dot(inner, inverse, precision=highest)
    first_row = (jnp.arange(width_all) == 0).astype(jnp.float32)[None, :]
    lower_rows = jnp.concatenate([weights[:, None], inverse.T], axis=1)
    return jnp.concatenate([first_row, lower_rows], axis=0)


def split(x):
    high = x.astype(BF16)
    return high, (x - high.astype(F32)).astype(BF16)


def window_kernel(
    n_lon, n_lat,
    prior, courant, survival, geometry, near_key, path_key, observed, obs_weight,
    end_out, gram_out,
    s0, s1, s2, s3, s4, s_high, s_low, paths, counts, h_high, h_low,
    near, beside, gram, packed, got_lat, part, got_lon, total, decay,
    load_sem, store_sem, west_send, west_recv, row_send, row_recv,
    ray_send, ray_recv, lat_send, lat_recv, lon_send, lon_recv, all_send, all_recv,
):
    lon = lax.axis_index("lon")
    lat = lax.axis_index("lat")

    def at_lon(d):
        return (lax.rem(lon + d + n_lon, n_lon), lat)

    def at_lat(d):
        return (lon, lax.rem(lat + d + n_lat, n_lat))

    has_low = lat > 0
    has_high = lat < n_lat - 1
    states = [s0, s1, s2, s3]

    loads = pltpu.make_async_copy(prior, s0.at[1:LON + 1, 1:LAT + 1], load_sem)
    loads.start()

    barrier = pltpu.get_barrier_semaphore()
    for d in range(1, n_lon):
        pl.semaphore_signal(barrier, inc=1, device_id=at_lon(d), device_id_type=MESH)
    for d in range(1, n_lat):
        pl.semaphore_signal(barrier, inc=1, device_id=at_lat(d), device_id_type=MESH)
    pl.semaphore_wait(barrier, n_lon + n_lat - 2)

    def remote(src, dst, send, recv, to):
        return pltpu.make_async_remote_copy(
            src_ref=src, dst_ref=dst, send_sem=send, recv_sem=recv, device_id=to, device_id_type=MESH
        )

    def west_copy(k):
        src = prior.at[LON - 1] if k == 0 else states[k].at[LON, 1:LAT + 1]
        return remote(src, states[k].at[0, 1:LAT + 1], west_send.at[k], west_recv.at[k], at_lon(1))

    def up_copy(k):
        src = prior.at[:, LAT - 1] if k == 0 else states[k].at[1:LON + 1, LAT]
        return remote(src, states[k].at[1:LON + 1, 0], row_send.at[k, 0], row_recv.at[k, 0], at_lat(1))

    def down_copy(k):
        src = prior.at[:, 0] if k == 0 else states[k].at[1:LON + 1, 1]
        return remote(src, states[k].at[1:LON + 1, LAT + 1], row_send.at[k, 1], row_recv.at[k, 1], at_lat(-1))

    def ray_up(k):
        return remote(near.at[k, 2], beside.at[k, 0], ray_send.at[k, 0], ray_recv.at[k, 0], at_lat(1))

    def ray_down(k):
        return remote(near.at[k, 0], beside.at[k, 1], ray_send.at[k, 1], ray_recv.at[k, 1], at_lat(-1))

    def send_rows(k):
        @pl.when(has_high)
        def _():
            up_copy(k).start()

        @pl.when(has_low)
        def _():
            down_copy(k).start()

    def send_rays(k):
        @pl.when(has_high)
        def _():
            ray_up(k).start()

        @pl.when(has_low)
        def _():
            ray_down(k).start()

    send_rows(0)
    west_copy(0).start()

    @pl.when(jnp.logical_not(has_low))
    def _():
        for k in range(STEPS):
            def clear(i, c, k=k):
                states[k][i + 1, 0] = jnp.zeros((ALT, WIDE), F32)
                return c
            lax.fori_loop(0, LON, clear, 0)
            beside[k, 0] = jnp.zeros((ROWS, WIDE), F32)

    @pl.when(jnp.logical_not(has_high))
    def _():
        for k in range(STEPS):
            def clear(i, c, k=k):
                states[k][i + 1, LAT + 1] = jnp.zeros((ALT, WIDE), F32)
                return c
            lax.fori_loop(0, LON, clear, 0)
            beside[k, 1] = jnp.zeros((ROWS, WIDE), F32)

    decay[...] = jnp.broadcast_to(survival[...], (ALT, WIDE))

    def turn(s, c):
        block = geometry[s]
        paths[s] = jnp.concatenate([block, block], axis=0).T
        return c

    lax.fori_loop(0, SEG, turn, 0)
    slots = near_key.shape[1]
    left = (lax.broadcasted_iota(jnp.int32, (NEAR * PAIRS, slots), 0) == near_key[...]).astype(F32).astype(BF16)
    half = lax.broadcasted_iota(jnp.int32, (slots, HALF), 1) // ALT
    for s in range(SEG):
        right = (half + 2 * s == path_key[...]).astype(F32).astype(BF16)
        counts[:, s] = jnp.dot(left, right, preferred_element_type=F32)

    def build_tile(t, c):
        def build(p, c2):
            row = t * PAIRS + p
            number = counts[row]
            total_path = number[0:1] * paths[0]
            for s in range(1, SEG):
                total_path += number[s:s + 1] * paths[s]
            high, low = split(total_path)
            at = (pl.ds(pl.multiple_of(t * RAYS, RAYS), RAYS), pl.ds(pl.multiple_of(p * HALF, HALF), HALF))
            h_high[at] = high
            h_low[at] = low
            return c2

        return lax.fori_loop(0, PAIRS, build, c)

    lax.fori_loop(0, NEAR, build_tile, 0)
    gram[...] = jnp.zeros((WIDE, WIDE), F32)

    def cell(k, i, j):
        old = states[k]
        drift = courant[i, j]
        keep = 1.0 - 2.0 * diffusion - drift
        new = keep * old[i + 1, j + 1] + drift * old[i, j + 1]
        new += diffusion * (old[i + 1, j + 2] + old[i + 1, j])
        new = new * decay[...]
        if k + 1 < STEPS:
            states[k + 1][i + 1, j + 1] = new
        else:
            s4[i, j] = new
        high, low = split(new)
        at = pl.ds(pl.multiple_of((i * LAT + j) * ALT, ALT), ALT)
        s_high[at] = high
        s_low[at] = low

    def cells(k, first, rows):
        def one(i, c):
            for j in rows:
                cell(k, i, j)
            return c

        lax.fori_loop(first, LON, one, 0)

    def project(k):
        def part_of(b, c):
            at = pl.ds(pl.multiple_of(b * 256, 256), 256)
            high, low = s_high[at], s_low[at]
            add = jnp.dot(h_high[:, at], high, preferred_element_type=F32)
            add += jnp.dot(h_high[:, at], low, preferred_element_type=F32)
            add += jnp.dot(h_low[:, at], high, preferred_element_type=F32)
            add = add.reshape(3, ROWS, WIDE)

            @pl.when(b == 0)
            def _():
                near[k] = add

            @pl.when(b > 0)
            def _():
                near[k] += add

            return c

        lax.fori_loop(0, LON * LAT * ALT // 256, part_of, 0)

    def add_gram(k):
        @pl.when(has_low)
        def _():
            ray_up(k).wait_recv()

        @pl.when(has_high)
        def _():
            ray_down(k).wait_recv()

        rays = near[k, 1] + beside[k, 0] + beside[k, 1]
        lane = lax.broadcasted_iota(jnp.int32, (ROWS, WIDE), 1)
        rays = jnp.where(lane == 0, observed[:, k:k + 1] - rays, rays) * obs_weight[:, k:k + 1]
        gram[...] += jnp.dot(rays.T, rays, precision=highest, preferred_element_type=F32)

    loads.wait()
    for k in range(STEPS):
        cells(k, 1, range(1, LAT - 1))
        west_copy(k).wait_recv()
        for j in range(1, LAT - 1):
            cell(k, 0, j)

        @pl.when(has_low)
        def _(k=k):
            up_copy(k).wait_recv()

        @pl.when(has_high)
        def _(k=k):
            down_copy(k).wait_recv()

        cells(k, 0, (0, LAT - 1))
        if k + 1 < STEPS:
            send_rows(k + 1)
            west_copy(k + 1).start()
        else:
            ends = pltpu.make_async_copy(s4, end_out, store_sem)
            ends.start()
        project(k)
        send_rays(k)
        if k > 0:
            add_gram(k - 1)
    add_gram(STEPS - 1)

    packed[0:WIDE] = gram[:, 0:HALF]
    packed[WIDE:PACKED] = gram[HALF:WIDE, HALF:WIDE]
    piece = PACKED // n_lat

    def own(index):
        return pl.ds(pl.multiple_of(index * piece, 8), piece)

    def scatter(d):
        to = lax.rem(lat + d, n_lat)
        return remote(packed.at[own(to)], got_lat.at[d], lat_send.at[d], lat_recv.at[d], at_lat(d))

    def across(d):
        return remote(part, got_lon.at[d], lon_send.at[d], lon_recv.at[d], at_lon(d))

    def gather(d):
        return remote(total.at[own(lat)], total.at[own(lat)], all_send.at[d], all_recv.at[d], at_lat(d))

    def landed(d):
        back = lax.rem(lat - d + n_lat, n_lat)
        return remote(total.at[own(back)], total.at[own(back)], all_send.at[d], all_recv.at[d], at_lat(d))

    for d in range(1, n_lat):
        scatter(d).start()
    acc = packed[own(lat)]
    for d in range(1, n_lat):
        scatter(d).wait_recv()
        acc += got_lat[d]
    part[...] = acc
    for d in range(1, n_lon):
        across(d).start()
    for d in range(1, n_lon):
        across(d).wait_recv()
        acc += got_lon[d]
    total[own(lat)] = acc
    for d in range(1, n_lat):
        gather(d).start()
    for d in range(1, n_lat):
        landed(d).wait_recv()
    gram_out[...] = total[...]

    for k in range(STEPS):
        west_copy(k).wait_send()

        @pl.when(has_high)
        def _(k=k):
            up_copy(k).wait_send()
            ray_up(k).wait_send()

        @pl.when(has_low)
        def _(k=k):
            down_copy(k).wait_send()
            ray_down(k).wait_send()

    for d in range(1, n_lat):
        scatter(d).wait_send()
        gather(d).wait_send()
    for d in range(1, n_lon):
        across(d).wait_send()
    ends.wait()


def window(n_lon, n_lat, *operands):
    piece = PACKED // n_lat
    ghosts = pltpu.VMEM((LON + 1, LAT + 2, ALT, WIDE), F32)
    cells_all = LON * LAT * ALT
    vmem = pl.BlockSpec(memory_space=pltpu.VMEM)
    smem = pl.BlockSpec(memory_space=pltpu.SMEM)
    hbm = pl.BlockSpec(memory_space=pl.ANY)
    dma = pltpu.SemaphoreType.DMA
    return pl.pallas_call(
        functools.partial(window_kernel, n_lon, n_lat),
        out_shape=(
            jax.ShapeDtypeStruct((LON, LAT, ALT, WIDE), F32),
            jax.ShapeDtypeStruct((PACKED, HALF), F32),
        ),
        in_specs=[hbm, smem, vmem, vmem, vmem, vmem, vmem, vmem],
        out_specs=(hbm, vmem),
        scratch_shapes=[
            ghosts, ghosts, ghosts, ghosts,
            pltpu.VMEM((LON, LAT, ALT, WIDE), F32),
            pltpu.VMEM((cells_all, WIDE), BF16),
            pltpu.VMEM((cells_all, WIDE), BF16),
            pltpu.VMEM((SEG, RAYS, HALF), F32),
            pltpu.VMEM((NEAR * PAIRS, SEG, HALF), F32),
            pltpu.VMEM((NEAR * RAYS, cells_all), BF16),
            pltpu.VMEM((NEAR * RAYS, cells_all), BF16),
            pltpu.VMEM((STEPS, 3, ROWS, WIDE), F32),
            pltpu.VMEM((STEPS, 2, ROWS, WIDE), F32),
            pltpu.VMEM((WIDE, WIDE), F32),
            pltpu.VMEM((PACKED, HALF), F32),
            pltpu.VMEM((n_lat, piece, HALF), F32),
            pltpu.VMEM((piece, HALF), F32),
            pltpu.VMEM((n_lon, piece, HALF), F32),
            pltpu.VMEM((PACKED, HALF), F32),
            pltpu.VMEM((ALT, WIDE), F32),
            dma, dma,
            dma((STEPS,)), dma((STEPS,)),
            dma((STEPS, 2)), dma((STEPS, 2)),
            dma((STEPS, 2)), dma((STEPS, 2)),
            dma((n_lat,)), dma((n_lat,)),
            dma((n_lon,)), dma((n_lon,)),
            dma((n_lat,)), dma((n_lat,)),
        ],
        compiler_params=pltpu.CompilerParams(
            collective_id=0, has_side_effects=True, vmem_limit_bytes=56 * 1024 * 1024
        ),
        cost_estimate=pl.CostEstimate(flops=12_000_000_000, bytes_accessed=6_000_000, transcendentals=0),
        name="window",
    )(*operands)


def shards(
    prior_state,
    courant,
    cell_survival_rate,
    geometry,
    entry_tile,
    entry_column,
    entry_segment,
    entry_counts,
    observed,
    obs_weight,
):
    n_lon, n_lat = lax.axis_size("lon"), lax.axis_size("lat")
    tiles_here = entry_tile[0, 0]
    columns_here = entry_column[0, 0]
    slot_total = tiles_here.shape[0]
    live_slot = jnp.arange(slot_total, dtype=jnp.int32) < entry_counts[0, 0]
    near_tile = tiles_here - (lax.axis_index("lat") - 1) * TILES
    near_key = jnp.where(live_slot, near_tile * PAIRS + columns_here // 2, -1)[None, :]
    path_key = (entry_segment[0, 0] * 2 + columns_here % 2)[:, None]
    end_forecast, packed = window(
        n_lon, n_lat,
        prior_state, courant, cell_survival_rate[:, None], geometry, near_key, path_key,
        observed.reshape(STEPS, ROWS).T, obs_weight.reshape(STEPS, ROWS).T,
    )
    upper = packed[HALF:WIDE].T
    gram_total = jnp.concatenate(
        [packed[:WIDE], jnp.concatenate([upper, packed[WIDE:]], axis=0)], axis=1
    )
    update = state_mapping(gram_total)
    end_state = jnp.dot(
        end_forecast.reshape(-1, WIDE), update, precision=highest
    ).reshape(prior_state.shape)
    start_state = jnp.dot(
        prior_state.reshape(-1, WIDE), update, precision=highest
    ).reshape(prior_state.shape)
    return (start_state, end_state)


def solution(mesh):
    placed = (
        P("lon", "lat", None, None),
        P("lon", "lat"),
        P(),
        P(),
        P("lon", "lat", None),
        P("lon", "lat", None),
        P("lon", "lat", None),
        P("lon", "lat"),
        P(None, "lon", "lat", None),
        P(None, "lon", "lat", None),
    )
    return jax.shard_map(
        shards,
        mesh=mesh,
        in_specs=placed,
        out_specs=(P("lon", "lat", None, None), P("lon", "lat", None, None)),
        check_vma=False,
    )
```

```python
import functools
import jax
import jax.numpy as jnp
from jax import lax
from jax.experimental import pallas as pl
from jax.experimental.pallas import tpu as pltpu
from jax.sharding import PartitionSpec as P

STEPS = 4
diffusion = 0.08
highest = lax.Precision.HIGHEST
MESH = pl.DeviceIdType.MESH
F32 = jnp.float32
BF16 = jnp.bfloat16

LON, LAT, ALT, WIDE = 8, 4, 64, 256
RAYS, SEG, TILES = 128, 16, 2
ROWS = TILES * RAYS
NEAR = 3 * TILES
PAIRS = LON * LAT // 2
HALF = 128
PACKED = WIDE + HALF
PANEL = 16
CELLS = LON * LAT * ALT
CHUNKS = 8


def split(x):
    high = x.astype(BF16)
    return high, (x - high.astype(F32)).astype(BF16)


def window_kernel(
    n_lon, n_lat,
    prior, courant, survival, geometry, entry_tile, entry_column, entry_segment, entry_counts,
    observed, obs_weight,
    prior_high, prior_low, end_high, end_low, gram_out,
    s0, s1, s2, s3, p_high, p_low, s_high, s_low, paths, counts, h_high, h_low,
    near, beside, gram, packed, got_lat, part, got_lon, total, decay, drifts, seen, scales,
    load_sem, store_sem, west_send, west_recv, row_send, row_recv,
    ray_send, ray_recv, lat_send, lat_recv, lon_send, lon_recv, all_send, all_recv,
):
    lon = lax.axis_index("lon")
    lat = lax.axis_index("lat")

    def at_lon(d):
        return (lax.rem(lon + d + n_lon, n_lon), lat)

    def at_lat(d):
        return (lon, lax.rem(lat + d + n_lat, n_lat))

    has_low = lat > 0
    has_high = lat < n_lat - 1
    states = [s0, s1, s2, s3]

    loads = pltpu.make_async_copy(prior, s0.at[1:LON + 1, 1:LAT + 1], load_sem)
    loads.start()

    barrier = pltpu.get_barrier_semaphore()
    for d in range(1, n_lon):
        pl.semaphore_signal(barrier, inc=1, device_id=at_lon(d), device_id_type=MESH)
    for d in range(1, n_lat):
        pl.semaphore_signal(barrier, inc=1, device_id=at_lat(d), device_id_type=MESH)
    pl.semaphore_wait(barrier, n_lon + n_lat - 2)

    def remote(src, dst, send, recv, to):
        return pltpu.make_async_remote_copy(
            src_ref=src, dst_ref=dst, send_sem=send, recv_sem=recv, device_id=to, device_id_type=MESH
        )

    def west_copy(k):
        src = prior.at[LON - 1] if k == 0 else states[k].at[LON, 1:LAT + 1]
        return remote(src, states[k].at[0, 1:LAT + 1], west_send.at[k], west_recv.at[k], at_lon(1))

    def up_copy(k):
        src = prior.at[:, LAT - 1] if k == 0 else states[k].at[1:LON + 1, LAT]
        return remote(src, states[k].at[1:LON + 1, 0], row_send.at[k, 0], row_recv.at[k, 0], at_lat(1))

    def down_copy(k):
        src = prior.at[:, 0] if k == 0 else states[k].at[1:LON + 1, 1]
        return remote(src, states[k].at[1:LON + 1, LAT + 1], row_send.at[k, 1], row_recv.at[k, 1], at_lat(-1))

    def ray_up(k):
        return remote(near.at[k, 2], beside.at[k, 0], ray_send.at[k, 0], ray_recv.at[k, 0], at_lat(1))

    def ray_down(k):
        return remote(near.at[k, 0], beside.at[k, 1], ray_send.at[k, 1], ray_recv.at[k, 1], at_lat(-1))

    def send_rows(k):
        @pl.when(has_high)
        def _():
            up_copy(k).start()

        @pl.when(has_low)
        def _():
            down_copy(k).start()

    def send_rays(k):
        @pl.when(has_high)
        def _():
            ray_up(k).start()

        @pl.when(has_low)
        def _():
            ray_down(k).start()

    send_rows(0)
    west_copy(0).start()

    @pl.when(jnp.logical_not(has_low))
    def _():
        for k in range(STEPS):
            def clear(i, c, k=k):
                states[k][i + 1, 0] = jnp.zeros((ALT, WIDE), F32)
                return c
            lax.fori_loop(0, LON, clear, 0)
            beside[k, 0] = jnp.zeros((ROWS, WIDE), F32)

    @pl.when(jnp.logical_not(has_high))
    def _():
        for k in range(STEPS):
            def clear(i, c, k=k):
                states[k][i + 1, LAT + 1] = jnp.zeros((ALT, WIDE), F32)
                return c
            lax.fori_loop(0, LON, clear, 0)
            beside[k, 1] = jnp.zeros((ROWS, WIDE), F32)

    def upright(line):
        return jnp.broadcast_to(line, (HALF, HALF)).T

    line = survival[...]
    line = upright(jnp.concatenate([line, line], axis=1))[0:ALT]
    decay[...] = jnp.concatenate([line, line], axis=1)
    for j in range(LAT):
        column = jnp.broadcast_to(courant[:, j:j + 1], (LON, WIDE))
        for i in range(LON):
            drifts[i, j] = jnp.broadcast_to(column[i:i + 1], (8, WIDE))
    for k in range(STEPS):
        for t in range(TILES):
            seen[k, t * RAYS:(t + 1) * RAYS] = upright(observed[k, 0, t:t + 1])
            scales[k, t * RAYS:(t + 1) * RAYS] = upright(obs_weight[k, 0, t:t + 1])

    def turn(s, c):
        block = geometry[s]
        paths[s] = jnp.concatenate([block, block], axis=0).T
        return c

    lax.fori_loop(0, SEG, turn, 0)
    slots = entry_tile.shape[2]
    column = entry_column[0]
    live = lax.broadcasted_iota(jnp.int32, (1, slots), 1) < entry_counts[...]
    near_key = (entry_tile[0] - (lat - 1) * TILES) * PAIRS + column // 2
    near_key = jnp.where(live, near_key, -1)
    path_key = entry_segment[0] * 2 + column % 2
    left = (lax.broadcasted_iota(jnp.int32, (NEAR * PAIRS, slots), 0) == near_key).astype(F32).astype(BF16)
    half = lax.broadcasted_iota(jnp.int32, (HALF, slots), 0) // ALT
    for s in range(SEG):
        right = (half + 2 * s == path_key).astype(F32).astype(BF16)
        counts[:, s] = lax.dot_general(
            left, right, (((1,), (1,)), ((), ())), preferred_element_type=F32
        )

    def build_tile(t, c):
        def build(p, c2):
            row = t * PAIRS + p
            number = counts[row]
            total_path = number[0:1] * paths[0]
            for s in range(1, SEG):
                total_path += number[s:s + 1] * paths[s]
            high, low = split(total_path)
            at = (pl.ds(pl.multiple_of(t * RAYS, RAYS), RAYS), pl.ds(pl.multiple_of(p * HALF, HALF), HALF))
            h_high[at] = high
            h_low[at] = low
            return c2

        return lax.fori_loop(0, PAIRS, build, c)

    lax.fori_loop(0, NEAR, build_tile, 0)
    gram[...] = jnp.zeros((WIDE, WIDE), F32)

    def cell(k, i, j):
        old = states[k]
        drift = drifts[i, j, 0:1]
        keep = 1.0 - 2.0 * diffusion - drift
        new = keep * old[i + 1, j + 1] + drift * old[i, j + 1]
        new += diffusion * (old[i + 1, j + 2] + old[i + 1, j])
        new = new * decay[...]
        if k + 1 < STEPS:
            states[k + 1][i + 1, j + 1] = new
        high, low = split(new)
        at = pl.ds(pl.multiple_of((i * LAT + j) * ALT, ALT), ALT)
        s_high[at] = high
        s_low[at] = low

    def cells(k, first, rows):
        def one(i, c):
            for j in rows:
                cell(k, i, j)
            return c

        lax.fori_loop(first, LON, one, 0)

    def project(k):
        def part_of(b, c):
            at = pl.ds(pl.multiple_of(b * 256, 256), 256)
            high, low = s_high[at], s_low[at]
            add = jnp.dot(h_high[:, at], high, preferred_element_type=F32)
            add += jnp.dot(h_high[:, at], low, preferred_element_type=F32)
            add += jnp.dot(h_low[:, at], high, preferred_element_type=F32)
            add = add.reshape(3, ROWS, WIDE)

            @pl.when(b == 0)
            def _():
                near[k] = add

            @pl.when(b > 0)
            def _():
                near[k] += add

            return c

        lax.fori_loop(0, LON * LAT * ALT // 256, part_of, 0)

    def add_gram(k):
        @pl.when(has_low)
        def _():
            ray_up(k).wait_recv()

        @pl.when(has_high)
        def _():
            ray_down(k).wait_recv()

        rays = near[k, 1] + beside[k, 0] + beside[k, 1]
        lane = lax.broadcasted_iota(jnp.int32, (ROWS, WIDE), 1)
        rays = jnp.where(lane == 0, jnp.concatenate([seen[k], seen[k]], axis=1) - rays, rays)
        rays = rays * jnp.concatenate([scales[k], scales[k]], axis=1)
        gram[...] += jnp.dot(rays.T, rays, precision=highest, preferred_element_type=F32)

    loads.wait()

    def split_prior(i, c):
        high, low = split(s0[i + 1, 1:LAT + 1].reshape(LAT * ALT, WIDE))
        at = pl.ds(pl.multiple_of(i * LAT * ALT, LAT * ALT), LAT * ALT)
        p_high[at] = high
        p_low[at] = low
        return c

    lax.fori_loop(0, LON, split_prior, 0)
    stores = [
        pltpu.make_async_copy(src, dst, store_sem.at[n])
        for n, (src, dst) in enumerate(
            ((p_high, prior_high), (p_low, prior_low), (s_high, end_high), (s_low, end_low))
        )
    ]
    for copy in stores[:2]:
        copy.start()
    for k in range(STEPS):
        cells(k, 1, range(1, LAT - 1))
        west_copy(k).wait_recv()
        for j in range(1, LAT - 1):
            cell(k, 0, j)

        @pl.when(has_low)
        def _(k=k):
            up_copy(k).wait_recv()

        @pl.when(has_high)
        def _(k=k):
            down_copy(k).wait_recv()

        cells(k, 0, (0, LAT - 1))
        if k + 1 < STEPS:
            send_rows(k + 1)
            west_copy(k + 1).start()
        else:
            for copy in stores[2:]:
                copy.start()
        project(k)
        send_rays(k)
        if k > 0:
            add_gram(k - 1)
    add_gram(STEPS - 1)

    packed[0:WIDE] = gram[:, 0:HALF]
    packed[WIDE:PACKED] = gram[HALF:WIDE, HALF:WIDE]
    piece = PACKED // n_lat

    def own(index):
        return pl.ds(pl.multiple_of(index * piece, 8), piece)

    def scatter(d):
        to = lax.rem(lat + d, n_lat)
        return remote(packed.at[own(to)], got_lat.at[d], lat_send.at[d], lat_recv.at[d], at_lat(d))

    def across(d):
        return remote(part, got_lon.at[d], lon_send.at[d], lon_recv.at[d], at_lon(d))

    def gather(d):
        return remote(total.at[own(lat)], total.at[own(lat)], all_send.at[d], all_recv.at[d], at_lat(d))

    def landed(d):
        back = lax.rem(lat - d + n_lat, n_lat)
        return remote(total.at[own(back)], total.at[own(back)], all_send.at[d], all_recv.at[d], at_lat(d))

    for d in range(1, n_lat):
        scatter(d).start()
    acc = packed[own(lat)]
    for d in range(1, n_lat):
        scatter(d).wait_recv()
        acc += got_lat[d]
    part[...] = acc
    for d in range(1, n_lon):
        across(d).start()
    for d in range(1, n_lon):
        across(d).wait_recv()
        acc += got_lon[d]
    total[own(lat)] = acc
    for d in range(1, n_lat):
        gather(d).start()
    for d in range(1, n_lat):
        landed(d).wait_recv()
    gram_out[...] = total[...]

    for k in range(STEPS):
        west_copy(k).wait_send()

        @pl.when(has_high)
        def _(k=k):
            up_copy(k).wait_send()
            ray_up(k).wait_send()

        @pl.when(has_low)
        def _(k=k):
            down_copy(k).wait_send()
            ray_down(k).wait_send()

    for d in range(1, n_lat):
        scatter(d).wait_send()
        gather(d).wait_send()
    for d in range(1, n_lon):
        across(d).wait_send()
    for copy in stores:
        copy.wait()


def window(n_lon, n_lat, *operands):
    piece = PACKED // n_lat
    ghosts = pltpu.VMEM((LON + 1, LAT + 2, ALT, WIDE), F32)
    half_type = jax.ShapeDtypeStruct((CELLS, WIDE), BF16)
    vmem = pl.BlockSpec(memory_space=pltpu.VMEM)
    hbm = pl.BlockSpec(memory_space=pl.ANY)
    dma = pltpu.SemaphoreType.DMA
    return pl.pallas_call(
        functools.partial(window_kernel, n_lon, n_lat),
        out_shape=(
            half_type, half_type, half_type, half_type,
            jax.ShapeDtypeStruct((PACKED, HALF), F32),
        ),
        in_specs=[hbm] + [vmem] * 9,
        out_specs=(hbm, hbm, hbm, hbm, vmem),
        scratch_shapes=[
            ghosts, ghosts, ghosts, ghosts,
            pltpu.VMEM((CELLS, WIDE), BF16),
            pltpu.VMEM((CELLS, WIDE), BF16),
            pltpu.VMEM((CELLS, WIDE), BF16),
            pltpu.VMEM((CELLS, WIDE), BF16),
            pltpu.VMEM((SEG, RAYS, HALF), F32),
            pltpu.VMEM((NEAR * PAIRS, SEG, HALF), F32),
            pltpu.VMEM((NEAR * RAYS, CELLS), BF16),
            pltpu.VMEM((NEAR * RAYS, CELLS), BF16),
            pltpu.VMEM((STEPS, 3, ROWS, WIDE), F32),
            pltpu.VMEM((STEPS, 2, ROWS, WIDE), F32),
            pltpu.VMEM((WIDE, WIDE), F32),
            pltpu.VMEM((PACKED, HALF), F32),
            pltpu.VMEM((n_lat, piece, HALF), F32),
            pltpu.VMEM((piece, HALF), F32),
            pltpu.VMEM((n_lon, piece, HALF), F32),
            pltpu.VMEM((PACKED, HALF), F32),
            pltpu.VMEM((ALT, WIDE), F32),
            pltpu.VMEM((LON, LAT, 8, WIDE), F32),
            pltpu.VMEM((STEPS, ROWS, HALF), F32),
            pltpu.VMEM((STEPS, ROWS, HALF), F32),
            dma, dma((4,)),
            dma((STEPS,)), dma((STEPS,)),
            dma((STEPS, 2)), dma((STEPS, 2)),
            dma((STEPS, 2)), dma((STEPS, 2)),
            dma((n_lat,)), dma((n_lat,)),
            dma((n_lon,)), dma((n_lon,)),
            dma((n_lat,)), dma((n_lat,)),
        ],
        compiler_params=pltpu.CompilerParams(
            collective_id=0, has_side_effects=True, vmem_limit_bytes=56 * 1024 * 1024
        ),
        cost_estimate=pl.CostEstimate(flops=12_000_000_000, bytes_accessed=6_000_000, transcendentals=0),
        name="window",
    )(*operands)


def panel_rows(block, at, rows_low, rows_high):
    spread = {}
    for j in range(PANEL):
        column = jnp.broadcast_to(block[:, at + j:at + j + 1], (PANEL, HALF))
        for i in range(j, PANEL):
            spread[i, j] = jnp.broadcast_to(column[i:i + 1], (8, HALF))
    rows = [
        [jnp.broadcast_to(part[i:i + 1], (8, HALF)) for part in (rows_low, rows_high)]
        for i in range(PANEL)
    ]
    for k in range(PANEL):
        scale = lax.rsqrt(spread[k, k])
        for i in range(k + 1, PANEL):
            spread[i, k] = spread[i, k] * scale
        rows[k] = [part * scale for part in rows[k]]
        for i in range(k + 1, PANEL):
            factor = spread[i, k]
            for j in range(k + 1, i + 1):
                spread[i, j] = spread[i, j] - factor * spread[j, k]
            rows[i] = [a - factor * b for a, b in zip(rows[i], rows[k])]
    return rows


def update_kernel(packed, prior_high, prior_low, end_high, end_low, start_out, end_out,
                  work, inverse, panel, u_high, u_low, z, results, load_sem, store_sem):
    sources = (prior_high, prior_low, end_high, end_low)
    loads = [pltpu.make_async_copy(src, z.at[n], load_sem.at[n]) for n, src in enumerate(sources)]
    for copy in loads:
        copy.start()

    lower = packed[0:WIDE]
    corner = lower[HALF:WIDE].T
    row = lax.broadcasted_iota(jnp.int32, (HALF, HALF), 0)
    lane = lax.broadcasted_iota(jnp.int32, (HALF, HALF), 1)
    same = (row == lane).astype(F32)
    inner = jnp.logical_and(row > 0, lane > 0)
    work[0:HALF, 0:HALF] = jnp.where(inner, lower[0:HALF], 0.0) + same
    work[0:HALF, HALF:WIDE] = jnp.where(row > 0, corner, 0.0)
    work[HALF:WIDE, 0:HALF] = jnp.where(lane > 0, lower[HALF:WIDE], 0.0)
    work[HALF:WIDE, HALF:WIDE] = packed[WIDE:PACKED] + same

    for p in range(WIDE // PANEL):
        first = p * PANEL
        side, at = first // HALF, first % HALF
        mine = slice(first, first + PANEL)
        lanes = lax.broadcasted_iota(jnp.int32, (PANEL, HALF), 1)
        rows_of = lax.broadcasted_iota(jnp.int32, (PANEL, HALF), 0)
        parts = [work[mine, 0:HALF], work[mine, HALF:WIDE]]
        block = parts[side]
        in_panel = jnp.logical_and(lanes >= at, lanes < at + PANEL)
        unit = (lanes == rows_of + at).astype(F32)
        if p == 0:
            right = jnp.logical_and(lanes == 0, rows_of > 0)
            unit = jnp.where(right, lower[mine], unit)
        parts[side] = jnp.where(in_panel, unit, block)
        rows = panel_rows(block, at, *parts)
        for i in range(PANEL):
            for h in range(2):
                panel[i:i + 1, h * HALF:(h + 1) * HALF] = rows[i][h][0:1]
        done = panel[...]
        wide = lax.broadcasted_iota(jnp.int32, (PANEL, WIDE), 1)
        inverse[mine] = jnp.where(wide < first + PANEL, done, 0.0)
        rest = first + PANEL
        if rest == WIDE:
            break
        high, low = split(done)
        left = jnp.concatenate([high, high, low], axis=0)
        both = jnp.concatenate([high, low, high], axis=0)
        begin = HALF if rest >= HALF else 0
        change = lax.dot_general(
            left[:, begin:], both, (((0,), (0,)), ((), ())), preferred_element_type=F32
        )
        old = work[rest:WIDE]
        wide = lax.broadcasted_iota(jnp.int32, (WIDE - rest, WIDE), 1)
        blank = jnp.logical_and(wide >= first, wide < rest)
        if p == 0:
            start = jnp.where(lane[0:1] == 0, lower[rest:WIDE], 0.0)
            start = jnp.concatenate([start, jnp.zeros_like(start)], axis=1)
            old = jnp.where(blank, start, old)
        else:
            old = jnp.where(blank, 0.0, old)
        work[rest:WIDE] = old - change[rest - begin:]

    whole = inverse[...]
    wide = lax.broadcasted_iota(jnp.int32, (WIDE, WIDE), 1)
    tall = lax.broadcasted_iota(jnp.int32, (WIDE, WIDE), 0)
    right = jnp.where(tall[:, 0:1] > 0, whole[:, 0:1], 0.0)
    whole = jnp.where(jnp.logical_and(wide == 0, tall > 0), 0.0, whole)
    weights = jnp.sum(right * whole, axis=0, keepdims=True)
    turned = jnp.where(tall == 0, whole + weights, whole)
    high, low = split(turned.T)
    u_high[...] = high
    u_low[...] = low

    for copy in loads:
        copy.wait()
    size = CELLS // CHUNKS
    stores = []
    for n, out in enumerate((start_out, end_out)):
        for b in range(CHUNKS):
            at = slice(b * size, (b + 1) * size)
            a_high, a_low = z[2 * n, at], z[2 * n + 1, at]
            value = jnp.dot(a_high, u_high[...], preferred_element_type=F32)
            value += jnp.dot(a_low, u_high[...], preferred_element_type=F32)
            value += jnp.dot(a_high, u_low[...], preferred_element_type=F32)
            results[n, at] = value
            copy = pltpu.make_async_copy(results.at[n, at], out.at[at], store_sem.at[n, b])
            copy.start()
            stores.append(copy)
    for copy in stores:
        copy.wait()


def apply_update(packed, prior_high, prior_low, end_high, end_low):
    vmem = pl.BlockSpec(memory_space=pltpu.VMEM)
    hbm = pl.BlockSpec(memory_space=pl.ANY)
    out = jax.ShapeDtypeStruct((CELLS, WIDE), F32)
    return pl.pallas_call(
        update_kernel,
        out_shape=(out, out),
        in_specs=[vmem, hbm, hbm, hbm, hbm],
        out_specs=(hbm, hbm),
        scratch_shapes=[
            pltpu.VMEM((WIDE, WIDE), F32),
            pltpu.VMEM((WIDE, WIDE), F32),
            pltpu.VMEM((PANEL, WIDE), F32),
            pltpu.VMEM((WIDE, WIDE), BF16),
            pltpu.VMEM((WIDE, WIDE), BF16),
            pltpu.VMEM((4, CELLS, WIDE), BF16),
            pltpu.VMEM((2, CELLS, WIDE), F32),
            pltpu.SemaphoreType.DMA((4,)),
            pltpu.SemaphoreType.DMA((2, CHUNKS)),
        ],
        compiler_params=pltpu.CompilerParams(vmem_limit_bytes=60 * 1024 * 1024),
        cost_estimate=pl.CostEstimate(flops=1_700_000_000, bytes_accessed=8_400_000, transcendentals=0),
        name="update",
    )(packed, prior_high, prior_low, end_high, end_low)


def shards(
    prior_state,
    courant,
    cell_survival_rate,
    geometry,
    entry_tile,
    entry_column,
    entry_segment,
    entry_counts,
    observed,
    obs_weight,
):
    n_lon, n_lat = lax.axis_size("lon"), lax.axis_size("lat")
    prior_high, prior_low, end_high, end_low, packed = window(
        n_lon, n_lat,
        prior_state, courant, cell_survival_rate[None, :], geometry,
        entry_tile, entry_column, entry_segment, entry_counts, observed, obs_weight,
    )
    start_state, end_state = apply_update(packed, prior_high, prior_low, end_high, end_low)
    return (start_state.reshape(prior_state.shape), end_state.reshape(prior_state.shape))


def solution(mesh):
    placed = (
        P("lon", "lat", None, None),
        P("lon", "lat"),
        P(),
        P(),
        P("lon", "lat", None),
        P("lon", "lat", None),
        P("lon", "lat", None),
        P("lon", "lat"),
        P(None, "lon", "lat", None),
        P(None, "lon", "lat", None),
    )
    return jax.shard_map(
        shards,
        mesh=mesh,
        in_specs=placed,
        out_specs=(P("lon", "lat", None, None), P("lon", "lat", None, None)),
        check_vma=False,
    )
```

```python
import functools
import jax
import jax.numpy as jnp
from jax import lax
from jax.experimental import pallas as pl
from jax.experimental.pallas import tpu as pltpu
from jax.sharding import PartitionSpec as P

STEPS = 4
diffusion = 0.08
highest = lax.Precision.HIGHEST
MESH = pl.DeviceIdType.MESH
F32 = jnp.float32
BF16 = jnp.bfloat16

LON, LAT, ALT, WIDE = 8, 4, 64, 256
RAYS, SEG, TILES = 128, 16, 2
ROWS = TILES * RAYS
NEAR = 3 * TILES
PAIRS = LON * LAT // 2
HALF = 128
PACKED = WIDE + HALF
PANEL = 16
CELLS = LON * LAT * ALT
CHUNKS = 8


def split(x):
    high = x.astype(BF16)
    return high, (x - high.astype(F32)).astype(BF16)


def window_kernel(
    n_lon, n_lat,
    prior, courant, survival, geometry, entry_tile, entry_column, entry_segment, entry_counts,
    observed, obs_weight,
    end_out, gram_out,
    s0, s1, s2, s3, s4, s_both, paths, counts, h_high, h_low,
    near, beside, turn_out, turn_in, gram, packed, got_lat, part, got_lon, total, decay, drifts, seen, scales,
    keys, drift_row,
    load_sem, store_sem, swap_send, swap_recv, small_send, small_recv, back_send, back_recv,
    west_send, west_recv, row_send, row_recv, ray_send, ray_recv, turn_send, turn_recv,
    lat_send, lat_recv, lon_send, lon_recv, all_send, all_recv,
):
    lon = lax.axis_index("lon")
    lat = lax.axis_index("lat")
    group = lax.div(lat, 4)
    mine = lax.rem(lax.div(lat, 2), 2)
    core = lax.rem(lat, 2)
    theirs = 1 - mine
    partner = (lon, lat + 2 - 4 * mine)
    states = [s0, s1, s2, s3]

    def at_lon(d):
        return (lax.rem(lon + d + n_lon, n_lon), lat)

    def at_lat(d):
        return (lon, lax.rem(lat + d + n_lat, n_lat))

    def band_of(slot):
        return 4 * group + 2 * slot + core

    def holder(band):
        to = (lon, 4 * lax.div(band, 4) + 2 * mine + lax.rem(band, 2))
        return to, lax.rem(lax.div(band, 2), 2)

    def has_up(slot):
        return band_of(slot) + 1 < n_lat

    def has_down(slot):
        return band_of(slot) > 0

    def remote(src, dst, send, recv, to):
        return pltpu.make_async_remote_copy(
            src_ref=src, dst_ref=dst, send_sem=send, recv_sem=recv, device_id=to, device_id_type=MESH
        )

    def half(index):
        return pl.ds(pl.multiple_of(index * HALF, HALF), HALF)

    cells_of = (slice(1, LON + 1), slice(1, LAT + 1))
    loads = pltpu.make_async_copy(prior.at[:, :, :, half(mine)], s0.at[(mine,) + cells_of], load_sem)
    loads.start()

    slots = entry_tile.shape[2]
    column = entry_column[0]
    live = lax.broadcasted_iota(jnp.int32, (1, slots), 1) < entry_counts[...]
    near_key = (entry_tile[0] - (lat - 1) * TILES) * PAIRS + column // 2
    near_key = jnp.where(live, near_key, -1)
    path_key = entry_segment[0] * 2 + column % 2
    keys[0, 0:1, 0:slots] = near_key
    keys[0, 1:2, 0:slots] = path_key
    drift_row[0] = jnp.broadcast_to(courant[:, 0:1], (LON, HALF))
    lanes = lax.broadcasted_iota(jnp.int32, (LON, HALF), 1)
    for j in range(1, LAT):
        drift_row[0] = jnp.where(lanes == j, jnp.broadcast_to(courant[:, j:j + 1], (LON, HALF)), drift_row[0])

    barrier = pltpu.get_barrier_semaphore()
    for d in range(1, n_lon):
        pl.semaphore_signal(barrier, inc=1, device_id=at_lon(d), device_id_type=MESH)
    for d in range(1, n_lat):
        pl.semaphore_signal(barrier, inc=1, device_id=at_lat(d), device_id_type=MESH)
    pl.semaphore_wait(barrier, n_lon + n_lat - 2)

    def swap():
        return remote(
            prior.at[:, :, :, half(theirs)], s0.at[(mine,) + cells_of], swap_send, swap_recv, partner
        )

    def swapped():
        return remote(
            prior.at[:, :, :, half(theirs)], s0.at[(theirs,) + cells_of], swap_send, swap_recv, partner
        )

    small = [
        remote(keys.at[0], keys.at[1], small_send.at[0], small_recv.at[0], partner),
        remote(drift_row.at[0], drift_row.at[1], small_send.at[1], small_recv.at[1], partner),
    ]
    for copy in small:
        copy.start()
    swap().start()

    def back():
        return remote(
            s4.at[theirs], end_out.at[:, :, :, half(mine)], back_send, back_recv, partner
        )

    def back_landed():
        return remote(
            s4.at[theirs], end_out.at[:, :, :, half(theirs)], back_send, back_recv, partner
        )

    def west_copy(k, s):
        state = states[k]
        return remote(
            state.at[s, LON, 1:LAT + 1], state.at[s, 0, 1:LAT + 1],
            west_send.at[k, s], west_recv.at[k, s], at_lon(1),
        )

    def row_copy(k, s, up):
        to, slot = holder(band_of(s) + (1 if up else -1))
        state = states[k]
        src = state.at[s, 1:LON + 1, LAT if up else 1]
        dst = state.at[slot, 1:LON + 1, 0 if up else LAT + 1]
        return remote(src, dst, row_send.at[k, s, up], row_recv.at[k, slot, up], to)

    def row_landed(k, s, up):
        state = states[k]
        ref = state.at[s, 1:LON + 1, 0 if up else LAT + 1]
        return remote(ref, ref, row_send.at[k, s, up], row_recv.at[k, s, up], partner)

    def ray_copy(k, s, up):
        to, slot = holder(band_of(s) + (1 if up else -1))
        return remote(
            near.at[k, s, 2 if up else 0], beside.at[k, slot, up],
            ray_send.at[k, s, up], ray_recv.at[k, slot, up], to,
        )

    def ray_landed(k, s, up):
        ref = beside.at[k, s, up]
        return remote(ref, ref, ray_send.at[k, s, up], ray_recv.at[k, s, up], partner)

    def turn_copy(k):
        return remote(turn_out.at[k], turn_in.at[k], turn_send.at[k], turn_recv.at[k], partner)

    def out_both(make, k, s, act):
        @pl.when(has_up(s))
        def _():
            act(make(k, s, 1))

        @pl.when(has_down(s))
        def _():
            act(make(k, s, 0))

    def in_both(make, k, s):
        @pl.when(has_down(s))
        def _():
            make(k, s, 1).wait_recv()

        @pl.when(has_up(s))
        def _():
            make(k, s, 0).wait_recv()

    def begin(copy):
        copy.start()

    def sent(copy):
        copy.wait_send()

    def send_edges(k, s):
        out_both(row_copy, k, s, begin)
        west_copy(k, s).start()

    loads.wait()
    send_edges(0, mine)

    for s, up, row, missing in ((0, 1, 0, has_down(0)), (1, 0, LAT + 1, has_up(1))):
        @pl.when(jnp.logical_not(missing))
        def _(s=s, up=up, row=row):
            for k in range(STEPS):
                def clear(i, c, k=k):
                    states[k][s, i + 1, row] = jnp.zeros((ALT, HALF), F32)
                    return c
                lax.fori_loop(0, LON, clear, 0)
                beside[k, s, up] = jnp.zeros((ROWS, HALF), F32)

    def upright(line):
        return jnp.broadcast_to(line, (HALF, HALF)).T

    line = survival[...]
    decay[...] = upright(jnp.concatenate([line, line], axis=1))[0:ALT]
    for k in range(STEPS):
        for t in range(TILES):
            seen[k, t * RAYS:(t + 1) * RAYS] = upright(observed[k, 0, t:t + 1])
            scales[k, t * RAYS:(t + 1) * RAYS] = upright(obs_weight[k, 0, t:t + 1])

    def turn_path(s, c):
        block = geometry[s]
        paths[s] = jnp.concatenate([block, block], axis=0).T
        return c

    lax.fori_loop(0, SEG, turn_path, 0)

    for copy in small:
        copy.wait_recv()
    wide_half = lax.broadcasted_iota(jnp.int32, (HALF, slots), 0) // ALT
    for slot in range(2):
        own = mine == slot
        at_key = jnp.where(own, keys[0, 0:1, 0:slots], keys[1, 0:1, 0:slots])
        by_path = jnp.where(own, keys[0, 1:2, 0:slots], keys[1, 1:2, 0:slots])
        left = (lax.broadcasted_iota(jnp.int32, (NEAR * PAIRS, slots), 0) == at_key).astype(F32).astype(BF16)
        for s in range(SEG):
            right = (wide_half + 2 * s == by_path).astype(F32).astype(BF16)
            counts[slot * NEAR * PAIRS:(slot + 1) * NEAR * PAIRS, s] = lax.dot_general(
                left, right, (((1,), (1,)), ((), ())), preferred_element_type=F32
            )
        drift_of = jnp.where(own, drift_row[0], drift_row[1])
        for j in range(LAT):
            across_lanes = jnp.broadcast_to(drift_of[:, j:j + 1], (LON, HALF))
            for i in range(LON):
                drifts[slot, i, j] = jnp.broadcast_to(across_lanes[i:i + 1], (8, HALF))

    def build_tile(t, c):
        def build(p, c2):
            number = counts[t * PAIRS + p]
            total_path = number[0:1] * paths[0]
            for s in range(1, SEG):
                total_path += number[s:s + 1] * paths[s]
            high, low = split(total_path)
            at = (pl.ds(pl.multiple_of(t * RAYS, RAYS), RAYS), half(p))
            h_high[at] = high
            h_low[at] = low
            return c2

        return lax.fori_loop(0, PAIRS, build, c)

    lax.fori_loop(0, 2 * NEAR, build_tile, 0)
    gram[...] = jnp.zeros((WIDE, WIDE), F32)

    def cell(k, s, i, j):
        old = states[k]
        drift = drifts[s, i, j, 0:1]
        keep = 1.0 - 2.0 * diffusion - drift
        new = keep * old[s, i + 1, j + 1] + drift * old[s, i, j + 1]
        new += diffusion * (old[s, i + 1, j + 2] + old[s, i + 1, j])
        new = new * decay[...]
        if k + 1 < STEPS:
            states[k + 1][s, i + 1, j + 1] = new
        else:
            s4[s, i, j] = new
        at = pl.ds(pl.multiple_of(((s * LON + i) * LAT + j) * ALT, ALT), ALT)
        high, low = split(new)
        s_both[at, 0:HALF] = high
        s_both[at, HALF:WIDE] = low

    def cells(k, first, last, rows):
        def one(n, c):
            s = lax.div(n, last - first)
            i = first + lax.rem(n, last - first)
            for j in rows:
                cell(k, s, i, j)
            return c

        lax.fori_loop(0, 2 * (last - first), one, 0)

    def project(k):
        for s in range(2):
            def part_of(b, c, s=s):
                at = pl.ds(pl.multiple_of(b * 256, 256), 256)
                both = s_both[pl.ds(pl.multiple_of(s * CELLS + b * 256, 256), 256)]
                rays = slice(s * NEAR * RAYS, (s + 1) * NEAR * RAYS)
                add = jnp.dot(h_high[rays, at], both, preferred_element_type=F32)
                add = add[:, 0:HALF] + add[:, HALF:WIDE]
                add += jnp.dot(h_low[rays, at], both[:, 0:HALF], preferred_element_type=F32)
                add = add.reshape(3, ROWS, HALF)

                @pl.when(b == 0)
                def _():
                    near[k, s] = add

                @pl.when(b > 0)
                def _():
                    near[k, s] += add

                return c

            lax.fori_loop(0, CELLS // 256, part_of, 0)
            out_both(ray_copy, k, s, begin)

    def turn(k):
        in_both(ray_landed, k, theirs)
        turn_out[k] = near[k, theirs, 1] + beside[k, theirs, 0] + beside[k, theirs, 1]
        turn_copy(k).start()

    def add_gram(k):
        in_both(ray_landed, k, mine)
        here = near[k, mine, 1] + beside[k, mine, 0] + beside[k, mine, 1]
        turn_copy(k).wait_recv()
        there = turn_in[k]
        first = mine == 0
        low = jnp.where(first, here, there)
        high = jnp.where(first, there, here)
        lane = lax.broadcasted_iota(jnp.int32, (ROWS, HALF), 1)
        low = jnp.where(lane == 0, seen[k] - low, low) * scales[k]
        high = high * scales[k]
        rays = jnp.concatenate([low, high], axis=1)
        gram[...] += jnp.dot(rays.T, rays, precision=highest, preferred_element_type=F32)

    swapped().wait_recv()
    send_edges(0, theirs)
    for k in range(STEPS):
        cells(k, 1, LON, range(1, LAT - 1))
        for s in range(2):
            west_copy(k, s).wait_recv()
        cells(k, 0, 1, range(1, LAT - 1))
        for s in range(2):
            in_both(row_landed, k, s)
        cells(k, 0, LON, (0, LAT - 1))
        if k + 1 < STEPS:
            for s in range(2):
                send_edges(k + 1, s)
        else:
            store = pltpu.make_async_copy(s4.at[mine], end_out.at[:, :, :, half(mine)], store_sem)
            store.start()
            back().start()
        if k > 0:
            turn(k - 1)
        project(k)
        if k > 1:
            add_gram(k - 2)
    add_gram(STEPS - 2)
    turn(STEPS - 1)
    add_gram(STEPS - 1)

    packed[0:WIDE] = gram[:, 0:HALF]
    packed[WIDE:PACKED] = gram[HALF:WIDE, HALF:WIDE]
    piece = PACKED // n_lat

    def own(index):
        return pl.ds(pl.multiple_of(index * piece, 8), piece)

    def scatter(d):
        to = lax.rem(lat + d, n_lat)
        return remote(packed.at[own(to)], got_lat.at[d], lat_send.at[d], lat_recv.at[d], at_lat(d))

    def across(d):
        return remote(part, got_lon.at[d], lon_send.at[d], lon_recv.at[d], at_lon(d))

    def gather(d):
        return remote(total.at[own(lat)], total.at[own(lat)], all_send.at[d], all_recv.at[d], at_lat(d))

    def landed(d):
        from_lat = lax.rem(lat - d + n_lat, n_lat)
        return remote(total.at[own(from_lat)], total.at[own(from_lat)], all_send.at[d], all_recv.at[d], at_lat(d))

    for d in range(1, n_lat):
        scatter(d).start()
    acc = packed[own(lat)]
    for d in range(1, n_lat):
        scatter(d).wait_recv()
        acc += got_lat[d]
    part[...] = acc
    for d in range(1, n_lon):
        across(d).start()
    for d in range(1, n_lon):
        across(d).wait_recv()
        acc += got_lon[d]
    total[own(lat)] = acc
    for d in range(1, n_lat):
        gather(d).start()
    for d in range(1, n_lat):
        landed(d).wait_recv()
    gram_out[...] = total[...]

    back_landed().wait_recv()
    store.wait()
    back().wait_send()
    swap().wait_send()
    for copy in small:
        copy.wait_send()
    for k in range(STEPS):
        turn_copy(k).wait_send()
        for s in range(2):
            west_copy(k, s).wait_send()
            out_both(row_copy, k, s, sent)
            out_both(ray_copy, k, s, sent)
    for d in range(1, n_lat):
        scatter(d).wait_send()
        gather(d).wait_send()
    for d in range(1, n_lon):
        across(d).wait_send()


def window(n_lon, n_lat, *operands):
    piece = PACKED // n_lat
    ghosts = pltpu.VMEM((2, LON + 1, LAT + 2, ALT, HALF), F32)
    vmem = pl.BlockSpec(memory_space=pltpu.VMEM)
    hbm = pl.BlockSpec(memory_space=pl.ANY)
    dma = pltpu.SemaphoreType.DMA
    return pl.pallas_call(
        functools.partial(window_kernel, n_lon, n_lat),
        out_shape=(
            jax.ShapeDtypeStruct((LON, LAT, ALT, WIDE), F32),
            jax.ShapeDtypeStruct((PACKED, HALF), F32),
        ),
        in_specs=[hbm] + [vmem] * 9,
        out_specs=(hbm, vmem),
        scratch_shapes=[
            ghosts, ghosts, ghosts, ghosts,
            pltpu.VMEM((2, LON, LAT, ALT, HALF), F32),
            pltpu.VMEM((2 * CELLS, WIDE), BF16),
            pltpu.VMEM((SEG, RAYS, HALF), F32),
            pltpu.VMEM((2 * NEAR * PAIRS, SEG, HALF), F32),
            pltpu.VMEM((2 * NEAR * RAYS, CELLS), BF16),
            pltpu.VMEM((2 * NEAR * RAYS, CELLS), BF16),
            pltpu.VMEM((STEPS, 2, 3, ROWS, HALF), F32),
            pltpu.VMEM((STEPS, 2, 2, ROWS, HALF), F32),
            pltpu.VMEM((STEPS, ROWS, HALF), F32),
            pltpu.VMEM((STEPS, ROWS, HALF), F32),
            pltpu.VMEM((WIDE, WIDE), F32),
            pltpu.VMEM((PACKED, HALF), F32),
            pltpu.VMEM((n_lat, piece, HALF), F32),
            pltpu.VMEM((piece, HALF), F32),
            pltpu.VMEM((n_lon, piece, HALF), F32),
            pltpu.VMEM((PACKED, HALF), F32),
            pltpu.VMEM((ALT, HALF), F32),
            pltpu.VMEM((2, LON, LAT, 8, HALF), F32),
            pltpu.VMEM((STEPS, ROWS, HALF), F32),
            pltpu.VMEM((STEPS, ROWS, HALF), F32),
            pltpu.VMEM((2, 8, HALF), jnp.int32),
            pltpu.VMEM((2, LON, HALF), F32),
            dma, dma, dma, dma, dma((2,)), dma((2,)), dma, dma,
            dma((STEPS, 2)), dma((STEPS, 2)),
            dma((STEPS, 2, 2)), dma((STEPS, 2, 2)),
            dma((STEPS, 2, 2)), dma((STEPS, 2, 2)),
            dma((STEPS,)), dma((STEPS,)),
            dma((n_lat,)), dma((n_lat,)),
            dma((n_lon,)), dma((n_lon,)),
            dma((n_lat,)), dma((n_lat,)),
        ],
        compiler_params=pltpu.CompilerParams(
            collective_id=0, has_side_effects=True, vmem_limit_bytes=60 * 1024 * 1024
        ),
        cost_estimate=pl.CostEstimate(flops=12_000_000_000, bytes_accessed=6_000_000, transcendentals=0),
        name="window",
    )(*operands)


def panel_rows(block, at, rows_low, rows_high):
    spread = {}
    for j in range(PANEL):
        column = jnp.broadcast_to(block[:, at + j:at + j + 1], (PANEL, HALF))
        for i in range(j, PANEL):
            spread[i, j] = jnp.broadcast_to(column[i:i + 1], (8, HALF))
    rows = [
        [jnp.broadcast_to(part[i:i + 1], (8, HALF)) for part in (rows_low, rows_high)]
        for i in range(PANEL)
    ]
    for k in range(PANEL):
        scale = lax.rsqrt(spread[k, k])
        for i in range(k + 1, PANEL):
            spread[i, k] = spread[i, k] * scale
        rows[k] = [part * scale for part in rows[k]]
        for i in range(k + 1, PANEL):
            factor = spread[i, k]
            for j in range(k + 1, i + 1):
                spread[i, j] = spread[i, j] - factor * spread[j, k]
            rows[i] = [a - factor * b for a, b in zip(rows[i], rows[k])]
    return rows


def update_kernel(packed, prior, end, start_out, end_out,
                  work, inverse, panel, u_high, u_low, z, results, load_sem, store_sem):
    sources = (prior, end)
    loads = [pltpu.make_async_copy(src, z.at[n], load_sem.at[n]) for n, src in enumerate(sources)]
    for copy in loads:
        copy.start()

    lower = packed[0:WIDE]
    corner = lower[HALF:WIDE].T
    row = lax.broadcasted_iota(jnp.int32, (HALF, HALF), 0)
    lane = lax.broadcasted_iota(jnp.int32, (HALF, HALF), 1)
    same = (row == lane).astype(F32)
    inner = jnp.logical_and(row > 0, lane > 0)
    work[0:HALF, 0:HALF] = jnp.where(inner, lower[0:HALF], 0.0) + same
    work[0:HALF, HALF:WIDE] = jnp.where(row > 0, corner, 0.0)
    work[HALF:WIDE, 0:HALF] = jnp.where(lane > 0, lower[HALF:WIDE], 0.0)
    work[HALF:WIDE, HALF:WIDE] = packed[WIDE:PACKED] + same

    for p in range(WIDE // PANEL):
        first = p * PANEL
        side, at = first // HALF, first % HALF
        mine = slice(first, first + PANEL)
        lanes = lax.broadcasted_iota(jnp.int32, (PANEL, HALF), 1)
        rows_of = lax.broadcasted_iota(jnp.int32, (PANEL, HALF), 0)
        parts = [work[mine, 0:HALF], work[mine, HALF:WIDE]]
        block = parts[side]
        in_panel = jnp.logical_and(lanes >= at, lanes < at + PANEL)
        unit = (lanes == rows_of + at).astype(F32)
        if p == 0:
            right = jnp.logical_and(lanes == 0, rows_of > 0)
            unit = jnp.where(right, lower[mine], unit)
        parts[side] = jnp.where(in_panel, unit, block)
        rows = panel_rows(block, at, *parts)
        for i in range(PANEL):
            for h in range(2):
                panel[i:i + 1, h * HALF:(h + 1) * HALF] = rows[i][h][0:1]
        done = panel[...]
        wide = lax.broadcasted_iota(jnp.int32, (PANEL, WIDE), 1)
        inverse[mine] = jnp.where(wide < first + PANEL, done, 0.0)
        rest = first + PANEL
        if rest == WIDE:
            break
        high, low = split(done)
        left = jnp.concatenate([high, high, low], axis=0)
        both = jnp.concatenate([high, low, high], axis=0)
        begin = HALF if rest >= HALF else 0
        change = lax.dot_general(
            left[:, begin:], both, (((0,), (0,)), ((), ())), preferred_element_type=F32
        )
        old = work[rest:WIDE]
        wide = lax.broadcasted_iota(jnp.int32, (WIDE - rest, WIDE), 1)
        blank = jnp.logical_and(wide >= first, wide < rest)
        if p == 0:
            start = jnp.where(lane[0:1] == 0, lower[rest:WIDE], 0.0)
            start = jnp.concatenate([start, jnp.zeros_like(start)], axis=1)
            old = jnp.where(blank, start, old)
        else:
            old = jnp.where(blank, 0.0, old)
        work[rest:WIDE] = old - change[rest - begin:]

    whole = inverse[...]
    wide = lax.broadcasted_iota(jnp.int32, (WIDE, WIDE), 1)
    tall = lax.broadcasted_iota(jnp.int32, (WIDE, WIDE), 0)
    right = jnp.where(tall[:, 0:1] > 0, whole[:, 0:1], 0.0)
    whole = jnp.where(jnp.logical_and(wide == 0, tall > 0), 0.0, whole)
    weights = jnp.sum(right * whole, axis=0, keepdims=True)
    turned = jnp.where(tall == 0, whole + weights, whole)
    high, low = split(turned.T)
    u_high[...] = high
    u_low[...] = low

    for copy in loads:
        copy.wait()
    size = CELLS // CHUNKS
    stores = []
    for n, out in enumerate((start_out, end_out)):
        for b in range(CHUNKS):
            at = slice(b * size, (b + 1) * size)
            a_high, a_low = split(z[n, at])
            value = jnp.dot(a_high, u_high[...], preferred_element_type=F32)
            value += jnp.dot(a_low, u_high[...], preferred_element_type=F32)
            value += jnp.dot(a_high, u_low[...], preferred_element_type=F32)
            results[n, at] = value
            copy = pltpu.make_async_copy(results.at[n, at], out.at[at], store_sem.at[n, b])
            copy.start()
            stores.append(copy)
    for copy in stores:
        copy.wait()


def apply_update(packed, prior, end):
    vmem = pl.BlockSpec(memory_space=pltpu.VMEM)
    hbm = pl.BlockSpec(memory_space=pl.ANY)
    out = jax.ShapeDtypeStruct((CELLS, WIDE), F32)
    return pl.pallas_call(
        update_kernel,
        out_shape=(out, out),
        in_specs=[vmem, hbm, hbm],
        out_specs=(hbm, hbm),
        scratch_shapes=[
            pltpu.VMEM((WIDE, WIDE), F32),
            pltpu.VMEM((WIDE, WIDE), F32),
            pltpu.VMEM((PANEL, WIDE), F32),
            pltpu.VMEM((WIDE, WIDE), BF16),
            pltpu.VMEM((WIDE, WIDE), BF16),
            pltpu.VMEM((2, CELLS, WIDE), F32),
            pltpu.VMEM((2, CELLS, WIDE), F32),
            pltpu.SemaphoreType.DMA((2,)),
            pltpu.SemaphoreType.DMA((2, CHUNKS)),
        ],
        compiler_params=pltpu.CompilerParams(vmem_limit_bytes=60 * 1024 * 1024),
        cost_estimate=pl.CostEstimate(flops=1_700_000_000, bytes_accessed=8_400_000, transcendentals=0),
        name="update",
    )(packed, prior, end)


def shards(
    prior_state,
    courant,
    cell_survival_rate,
    geometry,
    entry_tile,
    entry_column,
    entry_segment,
    entry_counts,
    observed,
    obs_weight,
):
    n_lon, n_lat = lax.axis_size("lon"), lax.axis_size("lat")
    forecast, packed = window(
        n_lon, n_lat,
        prior_state, courant, cell_survival_rate[None, :], geometry,
        entry_tile, entry_column, entry_segment, entry_counts, observed, obs_weight,
    )
    start_state, end_state = apply_update(
        packed, prior_state.reshape(CELLS, WIDE), forecast.reshape(CELLS, WIDE)
    )
    return (start_state.reshape(prior_state.shape), end_state.reshape(prior_state.shape))


def solution(mesh):
    placed = (
        P("lon", "lat", None, None),
        P("lon", "lat"),
        P(),
        P(),
        P("lon", "lat", None),
        P("lon", "lat", None),
        P("lon", "lat", None),
        P("lon", "lat"),
        P(None, "lon", "lat", None),
        P(None, "lon", "lat", None),
    )
    return jax.shard_map(
        shards,
        mesh=mesh,
        in_specs=placed,
        out_specs=(P("lon", "lat", None, None), P("lon", "lat", None, None)),
        check_vma=False,
    )
```

```python
import functools
import jax
import jax.numpy as jnp
from jax import lax
from jax.experimental import pallas as pl
from jax.experimental.pallas import tpu as pltpu
from jax.sharding import PartitionSpec as P

STEPS = 4
diffusion = 0.08
highest = lax.Precision.HIGHEST
MESH = pl.DeviceIdType.MESH
F32 = jnp.float32
BF16 = jnp.bfloat16

LON, LAT, ALT, WIDE = 8, 4, 64, 256
RAYS, SEG, TILES = 128, 16, 2
ROWS = TILES * RAYS
NEAR = 3 * TILES
PAIRS = LON * LAT // 2
HALF = 128
PACKED = WIDE + HALF
PANEL = 16
CELLS = LON * LAT * ALT
CHUNKS = 4
EARLY = 2


def split(x):
    high = x.astype(BF16)
    return high, (x - high.astype(F32)).astype(BF16)


def window_kernel(
    n_lon, n_lat,
    prior, courant, survival, geometry, entry_tile, entry_column, entry_segment, entry_counts,
    observed, obs_weight,
    end_out, u_high, u_low,
    s0, s1, s2, s3, s4, s_both, paths, counts, h_high, h_low,
    near, beside, turn_out, turn_in, gram, packed, got_lat, part, got_lon, total, decay, drifts, seen, scales,
    keys, drift_row, work, inverse, panel,
    load_sem, store_sem, swap_send, swap_recv, small_send, small_recv, back_send, back_recv,
    west_send, west_recv, row_send, row_recv, ray_send, ray_recv, turn_send, turn_recv,
    lat_send, lat_recv, lon_send, lon_recv, all_send, all_recv,
):
    lon = lax.axis_index("lon")
    lat = lax.axis_index("lat")
    group = lax.div(lat, 4)
    mine = lax.rem(lax.div(lat, 2), 2)
    core = lax.rem(lat, 2)
    theirs = 1 - mine
    partner = (lon, lat + 2 - 4 * mine)
    states = [s0, s1, s2, s3]

    def at_lon(d):
        return (lax.rem(lon + d + n_lon, n_lon), lat)

    def at_lat(d):
        return (lon, lax.rem(lat + d + n_lat, n_lat))

    def band_of(slot):
        return 4 * group + 2 * slot + core

    def holder(band):
        to = (lon, 4 * lax.div(band, 4) + 2 * mine + lax.rem(band, 2))
        return to, lax.rem(lax.div(band, 2), 2)

    def has_up(slot):
        return band_of(slot) + 1 < n_lat

    def has_down(slot):
        return band_of(slot) > 0

    def remote(src, dst, send, recv, to):
        return pltpu.make_async_remote_copy(
            src_ref=src, dst_ref=dst, send_sem=send, recv_sem=recv, device_id=to, device_id_type=MESH
        )

    def half(index):
        return pl.ds(pl.multiple_of(index * HALF, HALF), HALF)

    cells_of = (slice(1, LON + 1), slice(1, LAT + 1))
    loads = pltpu.make_async_copy(prior.at[:, :, :, half(mine)], s0.at[(mine,) + cells_of], load_sem)
    loads.start()

    slots = entry_tile.shape[2]
    column = entry_column[0]
    live = lax.broadcasted_iota(jnp.int32, (1, slots), 1) < entry_counts[...]
    near_key = (entry_tile[0] - (lat - 1) * TILES) * PAIRS + column // 2
    near_key = jnp.where(live, near_key, -1)
    path_key = entry_segment[0] * 2 + column % 2
    keys[0, 0:1, 0:slots] = near_key
    keys[0, 1:2, 0:slots] = path_key
    drift_row[0] = jnp.broadcast_to(courant[:, 0:1], (LON, HALF))
    lanes = lax.broadcasted_iota(jnp.int32, (LON, HALF), 1)
    for j in range(1, LAT):
        drift_row[0] = jnp.where(lanes == j, jnp.broadcast_to(courant[:, j:j + 1], (LON, HALF)), drift_row[0])

    barrier = pltpu.get_barrier_semaphore()
    for d in range(1, n_lon):
        pl.semaphore_signal(barrier, inc=1, device_id=at_lon(d), device_id_type=MESH)
    for d in range(1, n_lat):
        pl.semaphore_signal(barrier, inc=1, device_id=at_lat(d), device_id_type=MESH)
    pl.semaphore_wait(barrier, n_lon + n_lat - 2)

    def swap():
        return remote(
            prior.at[:, :, :, half(theirs)], s0.at[(mine,) + cells_of], swap_send, swap_recv, partner
        )

    def swapped():
        return remote(
            prior.at[:, :, :, half(theirs)], s0.at[(theirs,) + cells_of], swap_send, swap_recv, partner
        )

    small = [
        remote(keys.at[0], keys.at[1], small_send.at[0], small_recv.at[0], partner),
        remote(drift_row.at[0], drift_row.at[1], small_send.at[1], small_recv.at[1], partner),
    ]
    for copy in small:
        copy.start()
    swap().start()

    def back(i):
        return remote(
            s4.at[theirs, i], end_out.at[i, :, :, half(mine)], back_send.at[i], back_recv.at[i], partner
        )

    def back_landed(i):
        return remote(
            s4.at[theirs, i], end_out.at[i, :, :, half(theirs)], back_send.at[i], back_recv.at[i], partner
        )

    def west_copy(k, s):
        state = states[k]
        return remote(
            state.at[s, LON, 1:LAT + 1], state.at[s, 0, 1:LAT + 1],
            west_send.at[k, s], west_recv.at[k, s], at_lon(1),
        )

    def row_copy(k, s, up):
        to, slot = holder(band_of(s) + (1 if up else -1))
        state = states[k]
        src = state.at[s, 1:LON + 1, LAT if up else 1]
        dst = state.at[slot, 1:LON + 1, 0 if up else LAT + 1]
        return remote(src, dst, row_send.at[k, s, up], row_recv.at[k, slot, up], to)

    def row_landed(k, s, up):
        state = states[k]
        ref = state.at[s, 1:LON + 1, 0 if up else LAT + 1]
        return remote(ref, ref, row_send.at[k, s, up], row_recv.at[k, s, up], partner)

    def ray_copy(k, s, up):
        to, slot = holder(band_of(s) + (1 if up else -1))
        return remote(
            near.at[k, s, 2 if up else 0], beside.at[k, slot, up],
            ray_send.at[k, s, up], ray_recv.at[k, slot, up], to,
        )

    def ray_landed(k, s, up):
        ref = beside.at[k, s, up]
        return remote(ref, ref, ray_send.at[k, s, up], ray_recv.at[k, s, up], partner)

    def turn_copy(k):
        return remote(turn_out.at[k], turn_in.at[k], turn_send.at[k], turn_recv.at[k], partner)

    def out_both(make, k, s, act):
        @pl.when(has_up(s))
        def _():
            act(make(k, s, 1))

        @pl.when(has_down(s))
        def _():
            act(make(k, s, 0))

    def in_both(make, k, s):
        @pl.when(has_down(s))
        def _():
            make(k, s, 1).wait_recv()

        @pl.when(has_up(s))
        def _():
            make(k, s, 0).wait_recv()

    def begin(copy):
        copy.start()

    def sent(copy):
        copy.wait_send()

    def send_edges(k, s):
        out_both(row_copy, k, s, begin)
        west_copy(k, s).start()

    loads.wait()
    send_edges(0, mine)

    for s, up, row, missing in ((0, 1, 0, has_down(0)), (1, 0, LAT + 1, has_up(1))):
        @pl.when(jnp.logical_not(missing))
        def _(s=s, up=up, row=row):
            for k in range(STEPS):
                def clear(i, c, k=k):
                    states[k][s, i + 1, row] = jnp.zeros((ALT, HALF), F32)
                    return c
                lax.fori_loop(0, LON, clear, 0)
                beside[k, s, up] = jnp.zeros((ROWS, HALF), F32)

    def upright(line):
        return jnp.broadcast_to(line, (HALF, HALF)).T

    line = survival[...]
    decay[...] = upright(jnp.concatenate([line, line], axis=1))[0:ALT]
    for k in range(STEPS):
        for t in range(TILES):
            seen[k, t * RAYS:(t + 1) * RAYS] = upright(observed[k, 0, t:t + 1])
            scales[k, t * RAYS:(t + 1) * RAYS] = upright(obs_weight[k, 0, t:t + 1])

    def turn_path(s, c):
        block = geometry[s]
        paths[s] = jnp.concatenate([block, block], axis=0).T
        return c

    lax.fori_loop(0, SEG, turn_path, 0)

    for copy in small:
        copy.wait_recv()
    wide_half = lax.broadcasted_iota(jnp.int32, (HALF, slots), 0) // ALT
    for slot in range(2):
        own = mine == slot
        at_key = jnp.where(own, keys[0, 0:1, 0:slots], keys[1, 0:1, 0:slots])
        by_path = jnp.where(own, keys[0, 1:2, 0:slots], keys[1, 1:2, 0:slots])
        left = (lax.broadcasted_iota(jnp.int32, (NEAR * PAIRS, slots), 0) == at_key).astype(F32).astype(BF16)
        for s in range(SEG):
            right = (wide_half + 2 * s == by_path).astype(F32).astype(BF16)
            counts[slot * NEAR * PAIRS:(slot + 1) * NEAR * PAIRS, s] = lax.dot_general(
                left, right, (((1,), (1,)), ((), ())), preferred_element_type=F32
            )
        drift_of = jnp.where(own, drift_row[0], drift_row[1])
        for j in range(LAT):
            across_lanes = jnp.broadcast_to(drift_of[:, j:j + 1], (LON, HALF))
            for i in range(LON):
                drifts[slot, i, j] = jnp.broadcast_to(across_lanes[i:i + 1], (8, HALF))

    def build_tile(t, c):
        def build(p, c2):
            number = counts[t * PAIRS + p]
            total_path = number[0:1] * paths[0]
            for s in range(1, SEG):
                total_path += number[s:s + 1] * paths[s]
            high, low = split(total_path)
            at = (pl.ds(pl.multiple_of(t * RAYS, RAYS), RAYS), half(p))
            h_high[at] = high
            h_low[at] = low
            return c2

        return lax.fori_loop(0, PAIRS, build, c)

    lax.fori_loop(0, 2 * NEAR, build_tile, 0)
    gram[...] = jnp.zeros((WIDE, WIDE), F32)

    def cell(k, s, i, j):
        old = states[k]
        drift = drifts[s, i, j, 0:1]
        keep = 1.0 - 2.0 * diffusion - drift
        new = keep * old[s, i + 1, j + 1] + drift * old[s, i, j + 1]
        new += diffusion * (old[s, i + 1, j + 2] + old[s, i + 1, j])
        new = new * decay[...]
        if k + 1 < STEPS:
            states[k + 1][s, i + 1, j + 1] = new
        else:
            s4[s, i, j] = new
        at = pl.ds(pl.multiple_of(((s * LON + i) * LAT + j) * ALT, ALT), ALT)
        high, low = split(new)
        s_both[at, 0:HALF] = high
        s_both[at, HALF:WIDE] = low

    def cells(k, first, last, rows):
        def one(n, c):
            s = lax.div(n, last - first)
            i = first + lax.rem(n, last - first)
            for j in rows:
                cell(k, s, i, j)
            return c

        lax.fori_loop(0, 2 * (last - first), one, 0)

    def project(k):
        for s in range(2):
            def part_of(b, c, s=s):
                at = pl.ds(pl.multiple_of(b * 256, 256), 256)
                both = s_both[pl.ds(pl.multiple_of(s * CELLS + b * 256, 256), 256)]
                rays = slice(s * NEAR * RAYS, (s + 1) * NEAR * RAYS)
                add = jnp.dot(h_high[rays, at], both, preferred_element_type=F32)
                add = add[:, 0:HALF] + add[:, HALF:WIDE]
                add += jnp.dot(h_low[rays, at], both[:, 0:HALF], preferred_element_type=F32)
                add = add.reshape(3, ROWS, HALF)

                @pl.when(b == 0)
                def _():
                    near[k, s] = add

                @pl.when(b > 0)
                def _():
                    near[k, s] += add

                return c

            lax.fori_loop(0, CELLS // 256, part_of, 0)
            out_both(ray_copy, k, s, begin)

    def turn(k):
        in_both(ray_landed, k, theirs)
        turn_out[k] = near[k, theirs, 1] + beside[k, theirs, 0] + beside[k, theirs, 1]
        turn_copy(k).start()

    def add_gram(k):
        in_both(ray_landed, k, mine)
        here = near[k, mine, 1] + beside[k, mine, 0] + beside[k, mine, 1]
        turn_copy(k).wait_recv()
        there = turn_in[k]
        first = mine == 0
        low = jnp.where(first, here, there)
        high = jnp.where(first, there, here)
        lane = lax.broadcasted_iota(jnp.int32, (ROWS, HALF), 1)
        low = jnp.where(lane == 0, seen[k] - low, low) * scales[k]
        high = high * scales[k]
        rays = jnp.concatenate([low, high], axis=1)
        gram[...] += jnp.dot(rays.T, rays, precision=highest, preferred_element_type=F32)

    swapped().wait_recv()
    send_edges(0, theirs)
    for k in range(STEPS):
        cells(k, 1, LON, range(1, LAT - 1))
        for s in range(2):
            west_copy(k, s).wait_recv()
        cells(k, 0, 1, range(1, LAT - 1))
        for s in range(2):
            in_both(row_landed, k, s)
        cells(k, 0, LON, (0, LAT - 1))
        if k + 1 < STEPS:
            for s in range(2):
                send_edges(k + 1, s)
        else:
            store = pltpu.make_async_copy(s4.at[mine], end_out.at[:, :, :, half(mine)], store_sem)
            store.start()
            for i in range(EARLY):
                back(i).start()
        if k > 0:
            turn(k - 1)
        project(k)
        if k > 1:
            add_gram(k - 2)
    add_gram(STEPS - 2)
    turn(STEPS - 1)
    add_gram(STEPS - 1)

    packed[0:WIDE] = gram[:, 0:HALF]
    packed[WIDE:PACKED] = gram[HALF:WIDE, HALF:WIDE]
    piece = PACKED // n_lat

    def own(index):
        return pl.ds(pl.multiple_of(index * piece, 8), piece)

    def scatter(d):
        to = lax.rem(lat + d, n_lat)
        return remote(packed.at[own(to)], got_lat.at[d], lat_send.at[d], lat_recv.at[d], at_lat(d))

    def across(d):
        return remote(part, got_lon.at[d], lon_send.at[d], lon_recv.at[d], at_lon(d))

    def gather(d):
        return remote(total.at[own(lat)], total.at[own(lat)], all_send.at[d], all_recv.at[d], at_lat(d))

    def landed(d):
        from_lat = lax.rem(lat - d + n_lat, n_lat)
        return remote(total.at[own(from_lat)], total.at[own(from_lat)], all_send.at[d], all_recv.at[d], at_lat(d))

    for d in range(1, n_lat):
        scatter(d).start()
    acc = packed[own(lat)]
    for d in range(1, n_lat):
        scatter(d).wait_recv()
        acc += got_lat[d]
    part[...] = acc
    for d in range(1, n_lon):
        across(d).start()
    for d in range(1, n_lon):
        across(d).wait_recv()
        acc += got_lon[d]
    total[own(lat)] = acc
    for d in range(1, n_lat):
        gather(d).start()
    for d in range(1, n_lat):
        landed(d).wait_recv()
    for i in range(EARLY, LON):
        back(i).start()
    u_high[...], u_low[...] = update_matrix(total, work, inverse, panel)

    store.wait()
    for i in range(LON):
        back_landed(i).wait_recv()
        back(i).wait_send()
    swap().wait_send()
    for copy in small:
        copy.wait_send()
    for k in range(STEPS):
        turn_copy(k).wait_send()
        for s in range(2):
            west_copy(k, s).wait_send()
            out_both(row_copy, k, s, sent)
            out_both(ray_copy, k, s, sent)
    for d in range(1, n_lat):
        scatter(d).wait_send()
        gather(d).wait_send()
    for d in range(1, n_lon):
        across(d).wait_send()


def window(n_lon, n_lat, *operands):
    piece = PACKED // n_lat
    ghosts = pltpu.VMEM((2, LON + 1, LAT + 2, ALT, HALF), F32)
    vmem = pl.BlockSpec(memory_space=pltpu.VMEM)
    hbm = pl.BlockSpec(memory_space=pl.ANY)
    dma = pltpu.SemaphoreType.DMA
    return pl.pallas_call(
        functools.partial(window_kernel, n_lon, n_lat),
        out_shape=(
            jax.ShapeDtypeStruct((LON, LAT, ALT, WIDE), F32),
            jax.ShapeDtypeStruct((WIDE, WIDE), BF16),
            jax.ShapeDtypeStruct((WIDE, WIDE), BF16),
        ),
        in_specs=[hbm] + [vmem] * 9,
        out_specs=(hbm, vmem, vmem),
        scratch_shapes=[
            ghosts, ghosts, ghosts, ghosts,
            pltpu.VMEM((2, LON, LAT, ALT, HALF), F32),
            pltpu.VMEM((2 * CELLS, WIDE), BF16),
            pltpu.VMEM((SEG, RAYS, HALF), F32),
            pltpu.VMEM((2 * NEAR * PAIRS, SEG, HALF), F32),
            pltpu.VMEM((2 * NEAR * RAYS, CELLS), BF16),
            pltpu.VMEM((2 * NEAR * RAYS, CELLS), BF16),
            pltpu.VMEM((STEPS, 2, 3, ROWS, HALF), F32),
            pltpu.VMEM((STEPS, 2, 2, ROWS, HALF), F32),
            pltpu.VMEM((STEPS, ROWS, HALF), F32),
            pltpu.VMEM((STEPS, ROWS, HALF), F32),
            pltpu.VMEM((WIDE, WIDE), F32),
            pltpu.VMEM((PACKED, HALF), F32),
            pltpu.VMEM((n_lat, piece, HALF), F32),
            pltpu.VMEM((piece, HALF), F32),
            pltpu.VMEM((n_lon, piece, HALF), F32),
            pltpu.VMEM((PACKED, HALF), F32),
            pltpu.VMEM((ALT, HALF), F32),
            pltpu.VMEM((2, LON, LAT, 8, HALF), F32),
            pltpu.VMEM((STEPS, ROWS, HALF), F32),
            pltpu.VMEM((STEPS, ROWS, HALF), F32),
            pltpu.VMEM((2, 8, HALF), jnp.int32),
            pltpu.VMEM((2, LON, HALF), F32),
            pltpu.VMEM((WIDE, WIDE), F32),
            pltpu.VMEM((WIDE, WIDE), F32),
            pltpu.VMEM((PANEL, WIDE), F32),
            dma, dma, dma, dma, dma((2,)), dma((2,)), dma((LON,)), dma((LON,)),
            dma((STEPS, 2)), dma((STEPS, 2)),
            dma((STEPS, 2, 2)), dma((STEPS, 2, 2)),
            dma((STEPS, 2, 2)), dma((STEPS, 2, 2)),
            dma((STEPS,)), dma((STEPS,)),
            dma((n_lat,)), dma((n_lat,)),
            dma((n_lon,)), dma((n_lon,)),
            dma((n_lat,)), dma((n_lat,)),
        ],
        compiler_params=pltpu.CompilerParams(
            collective_id=0, has_side_effects=True, vmem_limit_bytes=60 * 1024 * 1024
        ),
        cost_estimate=pl.CostEstimate(flops=12_000_000_000, bytes_accessed=6_000_000, transcendentals=0),
        name="window",
    )(*operands)


def panel_rows(block, at, *parts):
    def spread(x):
        return jnp.broadcast_to(x[:, None, :], (x.shape[0], 8, HALF))

    columns = [
        spread(jnp.broadcast_to(block[:, at + j:at + j + 1], (PANEL, HALF))[j:]) for j in range(PANEL)
    ]
    parts = [spread(part) for part in parts]
    done = [[] for _ in parts]
    for k in range(PANEL):
        scale = lax.rsqrt(columns[k][0:1])
        factor = columns[k][1:] * scale
        for n, part in enumerate(parts):
            top = part[0:1] * scale
            done[n].append(top)
            if k + 1 < PANEL:
                parts[n] = part[1:] - factor * top
        for j in range(k + 1, PANEL):
            rest = factor[j - k - 1:]
            columns[j] = columns[j] - rest * rest[0:1]
    return done


def update_matrix(packed, work, inverse, panel):
    lower = packed[0:WIDE]
    corner = lower[HALF:WIDE].T
    row = lax.broadcasted_iota(jnp.int32, (HALF, HALF), 0)
    lane = lax.broadcasted_iota(jnp.int32, (HALF, HALF), 1)
    same = (row == lane).astype(F32)
    inner = jnp.logical_and(row > 0, lane > 0)
    work[0:HALF, 0:HALF] = jnp.where(inner, lower[0:HALF], 0.0) + same
    work[0:HALF, HALF:WIDE] = jnp.where(row > 0, corner, 0.0)
    work[HALF:WIDE, 0:HALF] = jnp.where(lane > 0, lower[HALF:WIDE], 0.0)
    work[HALF:WIDE, HALF:WIDE] = packed[WIDE:PACKED] + same

    for p in range(WIDE // PANEL):
        first = p * PANEL
        side, at = first // HALF, first % HALF
        mine = slice(first, first + PANEL)
        lanes = lax.broadcasted_iota(jnp.int32, (PANEL, HALF), 1)
        rows_of = lax.broadcasted_iota(jnp.int32, (PANEL, HALF), 0)
        parts = [work[mine, 0:HALF], work[mine, HALF:WIDE]]
        block = parts[side]
        in_panel = jnp.logical_and(lanes >= at, lanes < at + PANEL)
        unit = (lanes == rows_of + at).astype(F32)
        if p == 0:
            right = jnp.logical_and(lanes == 0, rows_of > 0)
            unit = jnp.where(right, lower[mine], unit)
        parts[side] = jnp.where(in_panel, unit, block)
        for h, done in enumerate(panel_rows(block, at, *parts)):
            for i in range(PANEL):
                panel[i:i + 1, h * HALF:(h + 1) * HALF] = done[i][0, 0:1]
        done = panel[...]
        wide = lax.broadcasted_iota(jnp.int32, (PANEL, WIDE), 1)
        inverse[mine] = jnp.where(wide < first + PANEL, done, 0.0)
        rest = first + PANEL
        if rest == WIDE:
            break
        high, low = split(done)
        left = jnp.concatenate([high, high, low], axis=0)
        both = jnp.concatenate([high, low, high], axis=0)
        begin = HALF if rest >= HALF else 0
        change = lax.dot_general(
            left[:, begin:], both, (((0,), (0,)), ((), ())), preferred_element_type=F32
        )
        old = work[rest:WIDE]
        wide = lax.broadcasted_iota(jnp.int32, (WIDE - rest, WIDE), 1)
        blank = jnp.logical_and(wide >= first, wide < rest)
        if p == 0:
            start = jnp.where(lane[0:1] == 0, lower[rest:WIDE], 0.0)
            start = jnp.concatenate([start, jnp.zeros_like(start)], axis=1)
            old = jnp.where(blank, start, old)
        else:
            old = jnp.where(blank, 0.0, old)
        work[rest:WIDE] = old - change[rest - begin:]

    whole = inverse[...]
    wide = lax.broadcasted_iota(jnp.int32, (WIDE, WIDE), 1)
    tall = lax.broadcasted_iota(jnp.int32, (WIDE, WIDE), 0)
    right = jnp.where(tall[:, 0:1] > 0, whole[:, 0:1], 0.0)
    whole = jnp.where(jnp.logical_and(wide == 0, tall > 0), 0.0, whole)
    weights = jnp.sum(right * whole, axis=0, keepdims=True)
    turned = jnp.where(tall == 0, whole + weights, whole)
    return split(turned.T)


def apply_kernel(u_high, u_low, prior, end, start_out, end_out, z, results, load_sem, store_sem):
    size = CELLS // CHUNKS
    pieces = [(n, b, slice(b * size, (b + 1) * size)) for n in range(2) for b in range(CHUNKS)]
    loads = [
        pltpu.make_async_copy((prior, end)[n].at[at], z.at[n, at], load_sem.at[n, b]) for n, b, at in pieces
    ]
    stores = [
        pltpu.make_async_copy(results.at[n, at], (start_out, end_out)[n].at[at], store_sem.at[n, b])
        for n, b, at in pieces
    ]
    for copy in loads:
        copy.start()
    for (n, b, at), load, store in zip(pieces, loads, stores):
        load.wait()
        a_high, a_low = split(z[n, at])
        value = jnp.dot(jnp.concatenate([a_high, a_low], axis=0), u_high[...], preferred_element_type=F32)
        value = value[:size] + value[size:]
        value += jnp.dot(a_high, u_low[...], preferred_element_type=F32)
        results[n, at] = value
        store.start()
    for copy in stores:
        copy.wait()


def apply_update(u_high, u_low, prior, end):
    vmem = pl.BlockSpec(memory_space=pltpu.VMEM)
    hbm = pl.BlockSpec(memory_space=pl.ANY)
    out = jax.ShapeDtypeStruct((CELLS, WIDE), F32)
    return pl.pallas_call(
        apply_kernel,
        out_shape=(out, out),
        in_specs=[vmem, vmem, hbm, hbm],
        out_specs=(hbm, hbm),
        scratch_shapes=[
            pltpu.VMEM((2, CELLS, WIDE), F32),
            pltpu.VMEM((2, CELLS, WIDE), F32),
            pltpu.SemaphoreType.DMA((2, CHUNKS)),
            pltpu.SemaphoreType.DMA((2, CHUNKS)),
        ],
        compiler_params=pltpu.CompilerParams(vmem_limit_bytes=60 * 1024 * 1024),
        cost_estimate=pl.CostEstimate(flops=1_700_000_000, bytes_accessed=8_400_000, transcendentals=0),
        name="update",
    )(u_high, u_low, prior, end)


def shards(
    prior_state,
    courant,
    cell_survival_rate,
    geometry,
    entry_tile,
    entry_column,
    entry_segment,
    entry_counts,
    observed,
    obs_weight,
):
    n_lon, n_lat = lax.axis_size("lon"), lax.axis_size("lat")
    forecast, u_high, u_low = window(
        n_lon, n_lat,
        prior_state, courant, cell_survival_rate[None, :], geometry,
        entry_tile, entry_column, entry_segment, entry_counts, observed, obs_weight,
    )
    start_state, end_state = apply_update(
        u_high, u_low, prior_state.reshape(CELLS, WIDE), forecast.reshape(CELLS, WIDE)
    )
    return (start_state.reshape(prior_state.shape), end_state.reshape(prior_state.shape))


def solution(mesh):
    placed = (
        P("lon", "lat", None, None),
        P("lon", "lat"),
        P(),
        P(),
        P("lon", "lat", None),
        P("lon", "lat", None),
        P("lon", "lat", None),
        P("lon", "lat"),
        P(None, "lon", "lat", None),
        P(None, "lon", "lat", None),
    )
    return jax.shard_map(
        shards,
        mesh=mesh,
        in_specs=placed,
        out_specs=(P("lon", "lat", None, None), P("lon", "lat", None, None)),
        check_vma=False,
    )
```

```python
import functools
import jax
import jax.numpy as jnp
from jax import lax
from jax.experimental import pallas as pl
from jax.experimental.pallas import tpu as pltpu
from jax.sharding import PartitionSpec as P

STEPS = 4
diffusion = 0.08
highest = lax.Precision.HIGHEST
MESH = pl.DeviceIdType.MESH
F32 = jnp.float32
BF16 = jnp.bfloat16

LON, LAT, ALT, WIDE = 8, 4, 64, 256
RAYS, SEG, TILES = 128, 16, 2
ROWS = TILES * RAYS
NEAR = 3 * TILES
PAIRS = LON * LAT // 2
HALF = 128
PACKED = WIDE + HALF
PANEL = 16
CELLS = LON * LAT * ALT
CHUNKS = 4
EARLY = 2
BESIDE_SCATTER = 3
BESIDE_ACROSS = 4
BESIDE_GATHER = 6


def split(x):
    high = x.astype(BF16)
    return high, (x - high.astype(F32)).astype(BF16)


def window_kernel(
    n_lon, n_lat,
    prior, courant, survival, geometry, entry_tile, entry_column, entry_segment, entry_counts,
    observed, obs_weight,
    end_out, u_high, u_low,
    s0, s1, s2, s3, s4, s_both, paths, counts, h_high, h_low,
    near, beside, turn_out, turn_in, gram, packed, got_lat, part, got_lon, total, decay, drifts, seen, scales,
    keys, drift_row, work, inverse, panel,
    load_sem, store_sem, swap_send, swap_recv, small_send, small_recv, back_send, back_recv,
    west_send, west_recv, row_send, row_recv, ray_send, ray_recv, turn_send, turn_recv,
    lat_send, lat_recv, lon_send, lon_recv, all_send, all_recv,
):
    lon = lax.axis_index("lon")
    lat = lax.axis_index("lat")
    group = lax.div(lat, 4)
    mine = lax.rem(lax.div(lat, 2), 2)
    core = lax.rem(lat, 2)
    theirs = 1 - mine
    partner = (lon, lat + 2 - 4 * mine)
    states = [s0, s1, s2, s3]

    def at_lon(d):
        return (lax.rem(lon + d + n_lon, n_lon), lat)

    def at_lat(d):
        return (lon, lax.rem(lat + d + n_lat, n_lat))

    def band_of(slot):
        return 4 * group + 2 * slot + core

    def holder(band):
        to = (lon, 4 * lax.div(band, 4) + 2 * mine + lax.rem(band, 2))
        return to, lax.rem(lax.div(band, 2), 2)

    def has_up(slot):
        return band_of(slot) + 1 < n_lat

    def has_down(slot):
        return band_of(slot) > 0

    def remote(src, dst, send, recv, to):
        return pltpu.make_async_remote_copy(
            src_ref=src, dst_ref=dst, send_sem=send, recv_sem=recv, device_id=to, device_id_type=MESH
        )

    def half(index):
        return pl.ds(pl.multiple_of(index * HALF, HALF), HALF)

    cells_of = (slice(1, LON + 1), slice(1, LAT + 1))
    loads = pltpu.make_async_copy(prior.at[:, :, :, half(mine)], s0.at[(mine,) + cells_of], load_sem)
    loads.start()

    slots = entry_tile.shape[2]
    column = entry_column[0]
    live = lax.broadcasted_iota(jnp.int32, (1, slots), 1) < entry_counts[...]
    near_key = (entry_tile[0] - (lat - 1) * TILES) * PAIRS + column // 2
    near_key = jnp.where(live, near_key, -1)
    path_key = entry_segment[0] * 2 + column % 2
    keys[0, 0:1, 0:slots] = near_key
    keys[0, 1:2, 0:slots] = path_key
    drift_row[0, 0:LAT, 0:LON] = courant[...]

    barrier = pltpu.get_barrier_semaphore()
    for d in range(1, n_lon):
        pl.semaphore_signal(barrier, inc=1, device_id=at_lon(d), device_id_type=MESH)
    for d in range(1, n_lat):
        pl.semaphore_signal(barrier, inc=1, device_id=at_lat(d), device_id_type=MESH)
    pl.semaphore_wait(barrier, n_lon + n_lat - 2)

    def swap():
        return remote(
            prior.at[:, :, :, half(theirs)], s0.at[(mine,) + cells_of], swap_send, swap_recv, partner
        )

    def swapped():
        return remote(
            prior.at[:, :, :, half(theirs)], s0.at[(theirs,) + cells_of], swap_send, swap_recv, partner
        )

    small = [
        remote(keys.at[0], keys.at[1], small_send.at[0], small_recv.at[0], partner),
        remote(drift_row.at[0], drift_row.at[1], small_send.at[1], small_recv.at[1], partner),
    ]
    for copy in small:
        copy.start()
    swap().start()

    def back(i):
        return remote(
            s4.at[theirs, i], end_out.at[i, :, :, half(mine)], back_send.at[i], back_recv.at[i], partner
        )

    def back_landed(i):
        return remote(
            s4.at[theirs, i], end_out.at[i, :, :, half(theirs)], back_send.at[i], back_recv.at[i], partner
        )

    def west_copy(k, s):
        state = states[k]
        return remote(
            state.at[s, LON, 1:LAT + 1], state.at[s, 0, 1:LAT + 1],
            west_send.at[k, s], west_recv.at[k, s], at_lon(1),
        )

    def row_copy(k, s, up):
        to, slot = holder(band_of(s) + (1 if up else -1))
        state = states[k]
        src = state.at[s, 1:LON + 1, LAT if up else 1]
        dst = state.at[slot, 1:LON + 1, 0 if up else LAT + 1]
        return remote(src, dst, row_send.at[k, s, up], row_recv.at[k, slot, up], to)

    def row_landed(k, s, up):
        state = states[k]
        ref = state.at[s, 1:LON + 1, 0 if up else LAT + 1]
        return remote(ref, ref, row_send.at[k, s, up], row_recv.at[k, s, up], partner)

    def ray_copy(k, s, up):
        to, slot = holder(band_of(s) + (1 if up else -1))
        return remote(
            near.at[k, s, 2 if up else 0], beside.at[k, slot, up],
            ray_send.at[k, s, up], ray_recv.at[k, slot, up], to,
        )

    def ray_landed(k, s, up):
        ref = beside.at[k, s, up]
        return remote(ref, ref, ray_send.at[k, s, up], ray_recv.at[k, s, up], partner)

    def turn_copy(k):
        return remote(turn_out.at[k], turn_in.at[k], turn_send.at[k], turn_recv.at[k], partner)

    def out_both(make, k, s, act):
        @pl.when(has_up(s))
        def _():
            act(make(k, s, 1))

        @pl.when(has_down(s))
        def _():
            act(make(k, s, 0))

    def in_both(make, k, s):
        @pl.when(has_down(s))
        def _():
            make(k, s, 1).wait_recv()

        @pl.when(has_up(s))
        def _():
            make(k, s, 0).wait_recv()

    def begin(copy):
        copy.start()

    def sent(copy):
        copy.wait_send()

    def send_edges(k, s):
        out_both(row_copy, k, s, begin)
        west_copy(k, s).start()

    loads.wait()
    send_edges(0, mine)

    for s, up, row, missing in ((0, 1, 0, has_down(0)), (1, 0, LAT + 1, has_up(1))):
        @pl.when(jnp.logical_not(missing))
        def _(s=s, up=up, row=row):
            for k in range(STEPS):
                def clear(i, c, k=k):
                    states[k][s, i + 1, row] = jnp.zeros((ALT, HALF), F32)
                    return c
                lax.fori_loop(0, LON, clear, 0)
                beside[k, s, up] = jnp.zeros((ROWS, HALF), F32)

    def upright(line):
        return jnp.broadcast_to(line, (HALF, HALF)).T

    line = survival[...]
    decay[...] = upright(jnp.concatenate([line, line], axis=1))[0:ALT]
    for k in range(STEPS):
        for t in range(TILES):
            seen[k, t * RAYS:(t + 1) * RAYS] = upright(observed[k, 0, t:t + 1])
            scales[k, t * RAYS:(t + 1) * RAYS] = upright(obs_weight[k, 0, t:t + 1])

    def turn_path(s, c):
        block = geometry[s]
        paths[s] = jnp.concatenate([block, block], axis=0).T
        return c

    lax.fori_loop(0, SEG, turn_path, 0)

    for copy in small:
        copy.wait_recv()
    wide_half = lax.broadcasted_iota(jnp.int32, (HALF, slots), 0) // ALT
    for slot in range(2):
        own = mine == slot
        at_key = jnp.where(own, keys[0, 0:1, 0:slots], keys[1, 0:1, 0:slots])
        by_path = jnp.where(own, keys[0, 1:2, 0:slots], keys[1, 1:2, 0:slots])
        left = (lax.broadcasted_iota(jnp.int32, (NEAR * PAIRS, slots), 0) == at_key).astype(F32).astype(BF16)
        for s in range(SEG):
            right = (wide_half + 2 * s == by_path).astype(F32).astype(BF16)
            counts[slot * NEAR * PAIRS:(slot + 1) * NEAR * PAIRS, s] = lax.dot_general(
                left, right, (((1,), (1,)), ((), ())), preferred_element_type=F32
            )
        drift_of = jnp.where(own, drift_row[0], drift_row[1])
        for i in range(LON):
            across_lanes = jnp.broadcast_to(drift_of[:, i:i + 1], (8, HALF))
            for j in range(LAT):
                drifts[slot, i, j] = jnp.broadcast_to(across_lanes[j:j + 1], (8, HALF))

    def build_tile(t, c):
        def build(p, c2):
            number = counts[t * PAIRS + p]
            total_path = number[0:1] * paths[0]
            for s in range(1, SEG):
                total_path += number[s:s + 1] * paths[s]
            high, low = split(total_path)
            at = (pl.ds(pl.multiple_of(t * RAYS, RAYS), RAYS), half(p))
            h_high[at] = high
            h_low[at] = low
            return c2

        return lax.fori_loop(0, PAIRS, build, c)

    lax.fori_loop(0, 2 * NEAR, build_tile, 0)
    gram[...] = jnp.zeros((WIDE, WIDE), F32)

    def cell(k, s, i, j):
        old = states[k]
        drift = drifts[s, i, j, 0:1]
        keep = 1.0 - 2.0 * diffusion - drift
        new = keep * old[s, i + 1, j + 1] + drift * old[s, i, j + 1]
        new += diffusion * (old[s, i + 1, j + 2] + old[s, i + 1, j])
        new = new * decay[...]
        if k + 1 < STEPS:
            states[k + 1][s, i + 1, j + 1] = new
        else:
            s4[s, i, j] = new
        at = pl.ds(pl.multiple_of(s * CELLS, CELLS) + (i * LAT + j) * ALT, ALT)
        high, low = split(new)
        s_both[at, 0:HALF] = high
        s_both[at, HALF:WIDE] = low

    def cells(k, first, last, rows):
        def one(s, c):
            for i in range(first, last):
                for j in rows:
                    cell(k, s, i, j)
            return c

        lax.fori_loop(0, 2, one, 0)

    def project(k):
        for s in range(2):
            def part_of(t, c, s=s):
                first = s * NEAR * RAYS + t * ROWS
                rays = pl.ds(pl.multiple_of(first, ROWS), ROWS)
                add = jnp.dot(h_high[rays], s_both[s * CELLS:(s + 1) * CELLS], preferred_element_type=F32)
                add = add[:, 0:HALF] + add[:, HALF:WIDE]
                add += jnp.dot(
                    h_low[rays], s_both[s * CELLS:(s + 1) * CELLS, 0:HALF], preferred_element_type=F32
                )
                near[k, s, t] = add
                return c

            lax.fori_loop(0, 3, part_of, 0)
            out_both(ray_copy, k, s, begin)

    def turn(k):
        in_both(ray_landed, k, theirs)
        turn_out[k] = near[k, theirs, 1] + beside[k, theirs, 0] + beside[k, theirs, 1]
        turn_copy(k).start()

    def add_gram(k):
        in_both(ray_landed, k, mine)
        here = near[k, mine, 1] + beside[k, mine, 0] + beside[k, mine, 1]
        turn_copy(k).wait_recv()
        there = turn_in[k]
        first = mine == 0
        low = jnp.where(first, here, there)
        high = jnp.where(first, there, here)
        lane = lax.broadcasted_iota(jnp.int32, (ROWS, HALF), 1)
        low = jnp.where(lane == 0, seen[k] - low, low) * scales[k]
        high = high * scales[k]
        rays = jnp.concatenate([low, high], axis=1)
        high, low = split(rays)
        left_high, left_low = split(rays.T)
        gram[...] += jnp.dot(
            jnp.concatenate([left_high, left_high, left_low], axis=1),
            jnp.concatenate([high, low, high], axis=0),
            preferred_element_type=F32,
        )

    swapped().wait_recv()
    send_edges(0, theirs)
    for k in range(STEPS):
        cells(k, 1, LON, range(1, LAT - 1))
        for s in range(2):
            west_copy(k, s).wait_recv()
        cells(k, 0, 1, range(1, LAT - 1))
        for s in range(2):
            in_both(row_landed, k, s)
        cells(k, 0, LON, (0, LAT - 1))
        if k + 1 < STEPS:
            for s in range(2):
                send_edges(k + 1, s)
        else:
            store = pltpu.make_async_copy(s4.at[mine], end_out.at[:, :, :, half(mine)], store_sem)
            store.start()
            for i in range(EARLY):
                back(i).start()
        if k > 0:
            turn(k - 1)
        project(k)
        if k > 1:
            add_gram(k - 2)
    add_gram(STEPS - 2)
    turn(STEPS - 1)
    add_gram(STEPS - 1)

    packed[0:WIDE] = gram[:, 0:HALF]
    packed[WIDE:PACKED] = gram[HALF:WIDE, HALF:WIDE]
    piece = PACKED // n_lat

    def own(index):
        return pl.ds(pl.multiple_of(index * piece, 8), piece)

    def scatter(d):
        to = lax.rem(lat + d, n_lat)
        return remote(packed.at[own(to)], got_lat.at[d], lat_send.at[d], lat_recv.at[d], at_lat(d))

    def across(d):
        return remote(part, got_lon.at[d], lon_send.at[d], lon_recv.at[d], at_lon(d))

    def gather(d):
        return remote(total.at[own(lat)], total.at[own(lat)], all_send.at[d], all_recv.at[d], at_lat(d))

    def landed(d):
        from_lat = lax.rem(lat - d + n_lat, n_lat)
        return remote(total.at[own(from_lat)], total.at[own(from_lat)], all_send.at[d], all_recv.at[d], at_lat(d))

    for d in range(1, n_lat):
        scatter(d).start()
    for i in range(EARLY, BESIDE_SCATTER):
        back(i).start()
    acc = packed[own(lat)]
    for d in range(1, n_lat):
        scatter(d).wait_recv()
        acc += got_lat[d]
    part[...] = acc
    for d in range(1, n_lon):
        across(d).start()
    for i in range(BESIDE_SCATTER, BESIDE_ACROSS):
        back(i).start()
    for d in range(1, n_lon):
        across(d).wait_recv()
        acc += got_lon[d]
    total[own(lat)] = acc
    for d in range(1, n_lat):
        gather(d).start()
    for i in range(BESIDE_ACROSS, BESIDE_GATHER):
        back(i).start()
    for d in range(1, n_lat):
        landed(d).wait_recv()
    for i in range(BESIDE_GATHER, LON):
        back(i).start()
    u_high[...], u_low[...] = update_matrix(total, work, inverse, panel)

    store.wait()
    for i in range(LON):
        back_landed(i).wait_recv()
        back(i).wait_send()
    swap().wait_send()
    for copy in small:
        copy.wait_send()
    for k in range(STEPS):
        turn_copy(k).wait_send()
        for s in range(2):
            west_copy(k, s).wait_send()
            out_both(row_copy, k, s, sent)
            out_both(ray_copy, k, s, sent)
    for d in range(1, n_lat):
        scatter(d).wait_send()
        gather(d).wait_send()
    for d in range(1, n_lon):
        across(d).wait_send()


def window(n_lon, n_lat, *operands):
    piece = PACKED // n_lat
    ghosts = pltpu.VMEM((2, LON + 1, LAT + 2, ALT, HALF), F32)
    vmem = pl.BlockSpec(memory_space=pltpu.VMEM)
    hbm = pl.BlockSpec(memory_space=pl.ANY)
    dma = pltpu.SemaphoreType.DMA
    return pl.pallas_call(
        functools.partial(window_kernel, n_lon, n_lat),
        out_shape=(
            jax.ShapeDtypeStruct((LON, LAT, ALT, WIDE), F32),
            jax.ShapeDtypeStruct((WIDE, WIDE), BF16),
            jax.ShapeDtypeStruct((WIDE, WIDE), BF16),
        ),
        in_specs=[hbm] + [vmem] * 9,
        out_specs=(hbm, vmem, vmem),
        scratch_shapes=[
            ghosts, ghosts, ghosts, ghosts,
            pltpu.VMEM((2, LON, LAT, ALT, HALF), F32),
            pltpu.VMEM((2 * CELLS, WIDE), BF16),
            pltpu.VMEM((SEG, RAYS, HALF), F32),
            pltpu.VMEM((2 * NEAR * PAIRS, SEG, HALF), F32),
            pltpu.VMEM((2 * NEAR * RAYS, CELLS), BF16),
            pltpu.VMEM((2 * NEAR * RAYS, CELLS), BF16),
            pltpu.VMEM((STEPS, 2, 3, ROWS, HALF), F32),
            pltpu.VMEM((STEPS, 2, 2, ROWS, HALF), F32),
            pltpu.VMEM((STEPS, ROWS, HALF), F32),
            pltpu.VMEM((STEPS, ROWS, HALF), F32),
            pltpu.VMEM((WIDE, WIDE), F32),
            pltpu.VMEM((PACKED, HALF), F32),
            pltpu.VMEM((n_lat, piece, HALF), F32),
            pltpu.VMEM((piece, HALF), F32),
            pltpu.VMEM((n_lon, piece, HALF), F32),
            pltpu.VMEM((PACKED, HALF), F32),
            pltpu.VMEM((ALT, HALF), F32),
            pltpu.VMEM((2, LON, LAT, 8, HALF), F32),
            pltpu.VMEM((STEPS, ROWS, HALF), F32),
            pltpu.VMEM((STEPS, ROWS, HALF), F32),
            pltpu.VMEM((2, 8, HALF), jnp.int32),
            pltpu.VMEM((2, 8, HALF), F32),
            pltpu.VMEM((WIDE, WIDE), F32),
            pltpu.VMEM((WIDE, WIDE), F32),
            pltpu.VMEM((PANEL, WIDE), F32),
            dma, dma, dma, dma, dma((2,)), dma((2,)), dma((LON,)), dma((LON,)),
            dma((STEPS, 2)), dma((STEPS, 2)),
            dma((STEPS, 2, 2)), dma((STEPS, 2, 2)),
            dma((STEPS, 2, 2)), dma((STEPS, 2, 2)),
            dma((STEPS,)), dma((STEPS,)),
            dma((n_lat,)), dma((n_lat,)),
            dma((n_lon,)), dma((n_lon,)),
            dma((n_lat,)), dma((n_lat,)),
        ],
        compiler_params=pltpu.CompilerParams(
            collective_id=0, has_side_effects=True, vmem_limit_bytes=60 * 1024 * 1024
        ),
        cost_estimate=pl.CostEstimate(flops=12_000_000_000, bytes_accessed=6_000_000, transcendentals=0),
        name="window",
    )(*operands)


def panel_rows(block, at, *parts):
    def spread(x):
        return jnp.broadcast_to(x[:, None, :], (x.shape[0], 8, HALF))

    columns = [
        spread(jnp.broadcast_to(block[:, at + j:at + j + 1], (PANEL, HALF))[j:]) for j in range(PANEL)
    ]
    parts = [spread(part) for part in parts]
    done = [[] for _ in parts]
    for k in range(PANEL):
        scale = lax.rsqrt(columns[k][0:1])
        factor = columns[k][1:] * scale
        for n, part in enumerate(parts):
            top = part[0:1] * scale
            done[n].append(top)
            if k + 1 < PANEL:
                parts[n] = part[1:] - factor * top
        for j in range(k + 1, PANEL):
            rest = factor[j - k - 1:]
            columns[j] = columns[j] - rest * rest[0:1]
    return done


def update_matrix(packed, work, inverse, panel):
    lower = packed[0:WIDE]
    corner = lower[HALF:WIDE].T
    row = lax.broadcasted_iota(jnp.int32, (HALF, HALF), 0)
    lane = lax.broadcasted_iota(jnp.int32, (HALF, HALF), 1)
    same = (row == lane).astype(F32)
    inner = jnp.logical_and(row > 0, lane > 0)
    work[0:HALF, 0:HALF] = jnp.where(inner, lower[0:HALF], 0.0) + same
    work[0:HALF, HALF:WIDE] = jnp.where(row > 0, corner, 0.0)
    work[HALF:WIDE, 0:HALF] = jnp.where(lane > 0, lower[HALF:WIDE], 0.0)
    work[HALF:WIDE, HALF:WIDE] = packed[WIDE:PACKED] + same

    for p in range(WIDE // PANEL):
        first = p * PANEL
        side, at = first // HALF, first % HALF
        mine = slice(first, first + PANEL)
        lanes = lax.broadcasted_iota(jnp.int32, (PANEL, HALF), 1)
        rows_of = lax.broadcasted_iota(jnp.int32, (PANEL, HALF), 0)
        parts = [work[mine, 0:HALF], work[mine, HALF:WIDE]]
        block = parts[side]
        in_panel = jnp.logical_and(lanes >= at, lanes < at + PANEL)
        unit = (lanes == rows_of + at).astype(F32)
        if p == 0:
            right = jnp.logical_and(lanes == 0, rows_of > 0)
            unit = jnp.where(right, lower[mine], unit)
        parts[side] = jnp.where(in_panel, unit, block)
        for h, done in enumerate(panel_rows(block, at, *parts)):
            for i in range(PANEL):
                panel[i:i + 1, h * HALF:(h + 1) * HALF] = done[i][0, 0:1]
        done = panel[...]
        wide = lax.broadcasted_iota(jnp.int32, (PANEL, WIDE), 1)
        inverse[mine] = jnp.where(wide < first + PANEL, done, 0.0)
        rest = first + PANEL
        if rest == WIDE:
            break
        high, low = split(done)
        left = jnp.concatenate([high, high, low], axis=0)
        both = jnp.concatenate([high, low, high], axis=0)
        begin = HALF if rest >= HALF else 0
        change = lax.dot_general(
            left[:, begin:], both, (((0,), (0,)), ((), ())), preferred_element_type=F32
        )
        old = work[rest:WIDE]
        wide = lax.broadcasted_iota(jnp.int32, (WIDE - rest, WIDE), 1)
        blank = jnp.logical_and(wide >= first, wide < rest)
        if p == 0:
            start = jnp.where(lane[0:1] == 0, lower[rest:WIDE], 0.0)
            start = jnp.concatenate([start, jnp.zeros_like(start)], axis=1)
            old = jnp.where(blank, start, old)
        else:
            old = jnp.where(blank, 0.0, old)
        work[rest:WIDE] = old - change[rest - begin:]

    whole = inverse[...]
    wide = lax.broadcasted_iota(jnp.int32, (WIDE, WIDE), 1)
    tall = lax.broadcasted_iota(jnp.int32, (WIDE, WIDE), 0)
    right = jnp.where(tall[:, 0:1] > 0, whole[:, 0:1], 0.0)
    whole = jnp.where(jnp.logical_and(wide == 0, tall > 0), 0.0, whole)
    weights = jnp.sum(right * whole, axis=0, keepdims=True)
    turned = jnp.where(tall == 0, whole + weights, whole)
    return split(turned.T)


def apply_kernel(u_high, u_low, prior, end, start_out, end_out, z, results, load_sem, store_sem):
    size = CELLS // CHUNKS
    pieces = [(n, b, slice(b * size, (b + 1) * size)) for n in range(2) for b in range(CHUNKS)]
    loads = [
        pltpu.make_async_copy((prior, end)[n].at[at], z.at[n, at], load_sem.at[n, b]) for n, b, at in pieces
    ]
    stores = [
        pltpu.make_async_copy(results.at[n, at], (start_out, end_out)[n].at[at], store_sem.at[n, b])
        for n, b, at in pieces
    ]
    for copy in loads:
        copy.start()
    for (n, b, at), load, store in zip(pieces, loads, stores):
        load.wait()
        a_high, a_low = split(z[n, at])
        value = jnp.dot(jnp.concatenate([a_high, a_low], axis=0), u_high[...], preferred_element_type=F32)
        value = value[:size] + value[size:]
        value += jnp.dot(a_high, u_low[...], preferred_element_type=F32)
        results[n, at] = value
        store.start()
    for copy in stores:
        copy.wait()


def apply_update(u_high, u_low, prior, end):
    vmem = pl.BlockSpec(memory_space=pltpu.VMEM)
    hbm = pl.BlockSpec(memory_space=pl.ANY)
    out = jax.ShapeDtypeStruct((CELLS, WIDE), F32)
    return pl.pallas_call(
        apply_kernel,
        out_shape=(out, out),
        in_specs=[vmem, vmem, hbm, hbm],
        out_specs=(hbm, hbm),
        scratch_shapes=[
            pltpu.VMEM((2, CELLS, WIDE), F32),
            pltpu.VMEM((2, CELLS, WIDE), F32),
            pltpu.SemaphoreType.DMA((2, CHUNKS)),
            pltpu.SemaphoreType.DMA((2, CHUNKS)),
        ],
        compiler_params=pltpu.CompilerParams(vmem_limit_bytes=60 * 1024 * 1024),
        cost_estimate=pl.CostEstimate(flops=1_700_000_000, bytes_accessed=8_400_000, transcendentals=0),
        name="update",
    )(u_high, u_low, prior, end)


def shards(
    prior_state,
    courant,
    cell_survival_rate,
    geometry,
    entry_tile,
    entry_column,
    entry_segment,
    entry_counts,
    observed,
    obs_weight,
):
    n_lon, n_lat = lax.axis_size("lon"), lax.axis_size("lat")
    forecast, u_high, u_low = window(
        n_lon, n_lat,
        prior_state, courant.T, cell_survival_rate[None, :], geometry,
        entry_tile, entry_column, entry_segment, entry_counts, observed, obs_weight,
    )
    start_state, end_state = apply_update(
        u_high, u_low, prior_state.reshape(CELLS, WIDE), forecast.reshape(CELLS, WIDE)
    )
    return (start_state.reshape(prior_state.shape), end_state.reshape(prior_state.shape))


def solution(mesh):
    placed = (
        P("lon", "lat", None, None),
        P("lon", "lat"),
        P(),
        P(),
        P("lon", "lat", None),
        P("lon", "lat", None),
        P("lon", "lat", None),
        P("lon", "lat"),
        P(None, "lon", "lat", None),
        P(None, "lon", "lat", None),
    )
    return jax.shard_map(
        shards,
        mesh=mesh,
        in_specs=placed,
        out_specs=(P("lon", "lat", None, None), P("lon", "lat", None, None)),
        check_vma=False,
    )
```

```python
import functools
import jax
import jax.numpy as jnp
from jax import lax
from jax.experimental import pallas as pl
from jax.experimental.pallas import tpu as pltpu
from jax.sharding import PartitionSpec as P

STEPS = 4
diffusion = 0.08
highest = lax.Precision.HIGHEST
MESH = pl.DeviceIdType.MESH
F32 = jnp.float32
BF16 = jnp.bfloat16

LON, LAT, ALT, WIDE = 8, 4, 64, 256
RAYS, SEG, TILES = 128, 16, 2
ROWS = TILES * RAYS
NEAR = 3 * TILES
PAIRS = LON * LAT // 2
HALF = 128
PACKED = WIDE + HALF
PANEL = 16
CELLS = LON * LAT * ALT
CHUNKS = 4
BUILD_FIRST = 7
EARLY = 2
BESIDE_SCATTER = 3
BESIDE_ACROSS = 4
BESIDE_GATHER = 6


def split(x):
    high = x.astype(BF16)
    return high, (x - high.astype(F32)).astype(BF16)


def window_kernel(
    n_lon, n_lat,
    prior, courant, survival, geometry, entry_tile, entry_column, entry_segment, entry_counts,
    observed, obs_weight,
    end_out, u_high, u_low,
    s0, s1, s2, s3, s4, s_both, paths, counts, h_high, h_low,
    near, beside, turn_out, turn_in, gram, packed, got_lat, part, got_lon, total, decay, drifts, seen, scales,
    keys, drift_row, work, inverse, panel,
    load_sem, store_sem, swap_send, swap_recv, small_send, small_recv, back_send, back_recv,
    west_send, west_recv, row_send, row_recv, ray_send, ray_recv, turn_send, turn_recv,
    lat_send, lat_recv, lon_send, lon_recv, all_send, all_recv,
):
    lon = lax.axis_index("lon")
    lat = lax.axis_index("lat")
    group = lax.div(lat, 4)
    mine = lax.rem(lax.div(lat, 2), 2)
    core = lax.rem(lat, 2)
    theirs = 1 - mine
    partner = (lon, lat + 2 - 4 * mine)
    states = [s0, s1, s2, s3]

    def at_lon(d):
        return (lax.rem(lon + d + n_lon, n_lon), lat)

    def at_lat(d):
        return (lon, lax.rem(lat + d + n_lat, n_lat))

    def band_of(slot):
        return 4 * group + 2 * slot + core

    def holder(band):
        to = (lon, 4 * lax.div(band, 4) + 2 * mine + lax.rem(band, 2))
        return to, lax.rem(lax.div(band, 2), 2)

    def has_up(slot):
        return band_of(slot) + 1 < n_lat

    def has_down(slot):
        return band_of(slot) > 0

    def remote(src, dst, send, recv, to):
        return pltpu.make_async_remote_copy(
            src_ref=src, dst_ref=dst, send_sem=send, recv_sem=recv, device_id=to, device_id_type=MESH
        )

    def half(index):
        return pl.ds(pl.multiple_of(index * HALF, HALF), HALF)

    cells_of = (slice(1, LON + 1), slice(1, LAT + 1))
    loads = pltpu.make_async_copy(prior.at[:, :, :, half(mine)], s0.at[(mine,) + cells_of], load_sem)
    loads.start()

    slots = entry_tile.shape[2]
    column = entry_column[0]
    live = lax.broadcasted_iota(jnp.int32, (1, slots), 1) < entry_counts[...]
    near_key = (entry_tile[0] - (lat - 1) * TILES) * PAIRS + column // 2
    near_key = jnp.where(live, near_key, -1)
    path_key = entry_segment[0] * 2 + column % 2
    keys[0, 0:1, 0:slots] = near_key
    keys[0, 1:2, 0:slots] = path_key
    drift_row[0, 0:LAT, 0:LON] = courant[...]

    barrier = pltpu.get_barrier_semaphore()
    for d in range(1, n_lon):
        pl.semaphore_signal(barrier, inc=1, device_id=at_lon(d), device_id_type=MESH)
    for d in range(1, n_lat):
        pl.semaphore_signal(barrier, inc=1, device_id=at_lat(d), device_id_type=MESH)
    pl.semaphore_wait(barrier, n_lon + n_lat - 2)

    swaps = ((0, LON, 0, 1), (0, LON, LAT - 1, LAT), (LON - 1, LON, 1, LAT - 1), (0, LON - 1, 1, LAT - 1))

    def swap(n, slot):
        i, i_end, j, j_end = swaps[n]
        return remote(
            prior.at[i:i_end, j:j_end, :, half(theirs)],
            s0.at[slot, i + 1:i_end + 1, j + 1:j_end + 1],
            swap_send.at[n], swap_recv.at[n], partner,
        )

    small = [
        remote(keys.at[0], keys.at[1], small_send.at[0], small_recv.at[0], partner),
        remote(drift_row.at[0], drift_row.at[1], small_send.at[1], small_recv.at[1], partner),
    ]
    for copy in small:
        copy.start()
    for n in range(len(swaps)):
        swap(n, mine).start()

    def back(i):
        return remote(
            s4.at[theirs, i], end_out.at[i, :, :, half(mine)], back_send.at[i], back_recv.at[i], partner
        )

    def back_landed(i):
        return remote(
            s4.at[theirs, i], end_out.at[i, :, :, half(theirs)], back_send.at[i], back_recv.at[i], partner
        )

    def west_copy(k, s):
        state = states[k]
        return remote(
            state.at[s, LON, 1:LAT + 1], state.at[s, 0, 1:LAT + 1],
            west_send.at[k, s], west_recv.at[k, s], at_lon(1),
        )

    def row_copy(k, s, up):
        to, slot = holder(band_of(s) + (1 if up else -1))
        state = states[k]
        src = state.at[s, 1:LON + 1, LAT if up else 1]
        dst = state.at[slot, 1:LON + 1, 0 if up else LAT + 1]
        return remote(src, dst, row_send.at[k, s, up], row_recv.at[k, slot, up], to)

    def row_landed(k, s, up):
        state = states[k]
        ref = state.at[s, 1:LON + 1, 0 if up else LAT + 1]
        return remote(ref, ref, row_send.at[k, s, up], row_recv.at[k, s, up], partner)

    def ray_copy(k, s, up):
        to, slot = holder(band_of(s) + (1 if up else -1))
        return remote(
            near.at[k, s, 2 if up else 0], beside.at[k, slot, up],
            ray_send.at[k, s, up], ray_recv.at[k, slot, up], to,
        )

    def ray_landed(k, s, up):
        ref = beside.at[k, s, up]
        return remote(ref, ref, ray_send.at[k, s, up], ray_recv.at[k, s, up], partner)

    def turn_copy(k):
        return remote(turn_out.at[k], turn_in.at[k], turn_send.at[k], turn_recv.at[k], partner)

    def out_both(make, k, s, act):
        @pl.when(has_up(s))
        def _():
            act(make(k, s, 1))

        @pl.when(has_down(s))
        def _():
            act(make(k, s, 0))

    def in_both(make, k, s):
        @pl.when(has_down(s))
        def _():
            make(k, s, 1).wait_recv()

        @pl.when(has_up(s))
        def _():
            make(k, s, 0).wait_recv()

    def begin(copy):
        copy.start()

    def sent(copy):
        copy.wait_send()

    def send_edges(k, s):
        out_both(row_copy, k, s, begin)
        west_copy(k, s).start()

    loads.wait()
    send_edges(0, mine)

    for s, up, row, missing in ((0, 1, 0, has_down(0)), (1, 0, LAT + 1, has_up(1))):
        @pl.when(jnp.logical_not(missing))
        def _(s=s, up=up, row=row):
            for k in range(STEPS):
                def clear(i, c, k=k):
                    states[k][s, i + 1, row] = jnp.zeros((ALT, HALF), F32)
                    return c
                lax.fori_loop(0, LON, clear, 0)
                beside[k, s, up] = jnp.zeros((ROWS, HALF), F32)

    def upright(line):
        return jnp.broadcast_to(line, (HALF, HALF)).T

    line = survival[...]
    decay[...] = upright(jnp.concatenate([line, line], axis=1))[0:ALT]
    for k in range(STEPS):
        for t in range(TILES):
            seen[k, t * RAYS:(t + 1) * RAYS] = upright(observed[k, 0, t:t + 1])
            scales[k, t * RAYS:(t + 1) * RAYS] = upright(obs_weight[k, 0, t:t + 1])

    def turn_path(s, c):
        block = geometry[s]
        paths[s] = jnp.concatenate([block, block], axis=0).T
        return c

    lax.fori_loop(0, SEG, turn_path, 0)

    for copy in small:
        copy.wait_recv()
    wide_half = lax.broadcasted_iota(jnp.int32, (HALF, slots), 0) // ALT
    for slot in range(2):
        own = mine == slot
        at_key = jnp.where(own, keys[0, 0:1, 0:slots], keys[1, 0:1, 0:slots])
        by_path = jnp.where(own, keys[0, 1:2, 0:slots], keys[1, 1:2, 0:slots])
        left = (lax.broadcasted_iota(jnp.int32, (NEAR * PAIRS, slots), 0) == at_key).astype(F32).astype(BF16)
        for s in range(SEG):
            right = (wide_half + 2 * s == by_path).astype(F32).astype(BF16)
            counts[slot * NEAR * PAIRS:(slot + 1) * NEAR * PAIRS, s] = lax.dot_general(
                left, right, (((1,), (1,)), ((), ())), preferred_element_type=F32
            )
        drift_of = jnp.where(own, drift_row[0], drift_row[1])
        for i in range(LON):
            across_lanes = jnp.broadcast_to(drift_of[:, i:i + 1], (8, HALF))
            for j in range(LAT):
                drifts[slot, i, j] = jnp.broadcast_to(across_lanes[j:j + 1], (8, HALF))

    def build_tile(t, c):
        def build(p, c2):
            number = counts[t * PAIRS + p]
            total_path = number[0:1] * paths[0]
            for s in range(1, SEG):
                total_path += number[s:s + 1] * paths[s]
            high, low = split(total_path)
            at = (pl.ds(pl.multiple_of(t * RAYS, RAYS), RAYS), half(p))
            h_high[at] = high
            h_low[at] = low
            return c2

        return lax.fori_loop(0, PAIRS, build, c)

    lax.fori_loop(0, BUILD_FIRST, build_tile, 0)
    for n in range(3):
        swap(n, theirs).wait_recv()
    send_edges(0, theirs)
    lax.fori_loop(BUILD_FIRST, 2 * NEAR, build_tile, 0)
    gram[...] = jnp.zeros((WIDE, WIDE), F32)

    def cell(k, s, i, j):
        old = states[k]
        drift = drifts[s, i, j, 0:1]
        keep = 1.0 - 2.0 * diffusion - drift
        new = keep * old[s, i + 1, j + 1] + drift * old[s, i, j + 1]
        new += diffusion * (old[s, i + 1, j + 2] + old[s, i + 1, j])
        new = new * decay[...]
        if k + 1 < STEPS:
            states[k + 1][s, i + 1, j + 1] = new
        else:
            s4[s, i, j] = new
        at = pl.ds(pl.multiple_of(s * CELLS, CELLS) + (i * LAT + j) * ALT, ALT)
        high, low = split(new)
        s_both[at, 0:HALF] = high
        s_both[at, HALF:WIDE] = low

    def cells(k, first, last, rows):
        def one(s, c):
            for i in range(first, last):
                for j in rows:
                    cell(k, s, i, j)
            return c

        lax.fori_loop(0, 2, one, 0)

    def project(k):
        for s, begin_at, step, number in ((0, 0, 2, 2), (1, 0, 2, 2), (0, 1, 0, 1), (1, 1, 0, 1)):
            def part_of(n, c, s=s, begin_at=begin_at, step=step):
                t = begin_at + step * n
                first = s * NEAR * RAYS + t * ROWS
                rays = pl.ds(pl.multiple_of(first, ROWS), ROWS)
                add = jnp.dot(h_high[rays], s_both[s * CELLS:(s + 1) * CELLS], preferred_element_type=F32)
                add = add[:, 0:HALF] + add[:, HALF:WIDE]
                add += jnp.dot(
                    h_low[rays], s_both[s * CELLS:(s + 1) * CELLS, 0:HALF], preferred_element_type=F32
                )
                near[k, s, t] = add
                return c

            lax.fori_loop(0, number, part_of, 0)
            if step:
                out_both(ray_copy, k, s, begin)

    def turn(k):
        in_both(ray_landed, k, theirs)
        turn_out[k] = near[k, theirs, 1] + beside[k, theirs, 0] + beside[k, theirs, 1]
        turn_copy(k).start()

    def add_gram(k):
        in_both(ray_landed, k, mine)
        here = near[k, mine, 1] + beside[k, mine, 0] + beside[k, mine, 1]
        turn_copy(k).wait_recv()
        there = turn_in[k]
        first = mine == 0
        low = jnp.where(first, here, there)
        high = jnp.where(first, there, here)
        lane = lax.broadcasted_iota(jnp.int32, (ROWS, HALF), 1)
        low = jnp.where(lane == 0, seen[k] - low, low) * scales[k]
        high = high * scales[k]
        rays = jnp.concatenate([low, high], axis=1)
        high, low = split(rays)
        left_high, left_low = split(rays.T)
        gram[...] += jnp.dot(
            jnp.concatenate([left_high, left_high, left_low], axis=1),
            jnp.concatenate([high, low, high], axis=0),
            preferred_element_type=F32,
        )

    swap(3, theirs).wait_recv()
    for k in range(STEPS):
        cells(k, 1, LON, range(1, LAT - 1))
        for s in range(2):
            west_copy(k, s).wait_recv()
        cells(k, 0, 1, range(1, LAT - 1))
        for s in range(2):
            in_both(row_landed, k, s)
        cells(k, 0, LON, (0, LAT - 1))
        if k + 1 < STEPS:
            for s in range(2):
                send_edges(k + 1, s)
        else:
            store = pltpu.make_async_copy(s4.at[mine], end_out.at[:, :, :, half(mine)], store_sem)
            store.start()
            for i in range(EARLY):
                back(i).start()
        if k > 0:
            turn(k - 1)
        project(k)
        if 1 < k < STEPS - 1:
            add_gram(k - 2)
    turn(STEPS - 1)
    for k in range(STEPS - 3, STEPS):
        add_gram(k)

    packed[0:WIDE] = gram[:, 0:HALF]
    packed[WIDE:PACKED] = gram[HALF:WIDE, HALF:WIDE]
    piece = PACKED // n_lat

    def own(index):
        return pl.ds(pl.multiple_of(index * piece, 8), piece)

    def scatter(d):
        to = lax.rem(lat + d, n_lat)
        return remote(packed.at[own(to)], got_lat.at[d], lat_send.at[d], lat_recv.at[d], at_lat(d))

    def across(d):
        return remote(part, got_lon.at[d], lon_send.at[d], lon_recv.at[d], at_lon(d))

    def gather(d):
        return remote(total.at[own(lat)], total.at[own(lat)], all_send.at[d], all_recv.at[d], at_lat(d))

    def landed(d):
        from_lat = lax.rem(lat - d + n_lat, n_lat)
        return remote(total.at[own(from_lat)], total.at[own(from_lat)], all_send.at[d], all_recv.at[d], at_lat(d))

    for d in range(1, n_lat):
        scatter(d).start()
    for i in range(EARLY, BESIDE_SCATTER):
        back(i).start()
    acc = packed[own(lat)]
    for d in range(1, n_lat):
        scatter(d).wait_recv()
        acc += got_lat[d]
    part[...] = acc
    for d in range(1, n_lon):
        across(d).start()
    for i in range(BESIDE_SCATTER, BESIDE_ACROSS):
        back(i).start()
    for d in range(1, n_lon):
        across(d).wait_recv()
        acc += got_lon[d]
    total[own(lat)] = acc
    for d in range(1, n_lat):
        gather(d).start()
    for i in range(BESIDE_ACROSS, BESIDE_GATHER):
        back(i).start()
    for d in range(1, n_lat):
        landed(d).wait_recv()
    for i in range(BESIDE_GATHER, LON):
        back(i).start()
    u_high[...], u_low[...] = update_matrix(total, work, inverse, panel)

    store.wait()
    for i in range(LON):
        back_landed(i).wait_recv()
        back(i).wait_send()
    for n in range(len(swaps)):
        swap(n, mine).wait_send()
    for copy in small:
        copy.wait_send()
    for k in range(STEPS):
        turn_copy(k).wait_send()
        for s in range(2):
            west_copy(k, s).wait_send()
            out_both(row_copy, k, s, sent)
            out_both(ray_copy, k, s, sent)
    for d in range(1, n_lat):
        scatter(d).wait_send()
        gather(d).wait_send()
    for d in range(1, n_lon):
        across(d).wait_send()


def window(n_lon, n_lat, *operands):
    piece = PACKED // n_lat
    ghosts = pltpu.VMEM((2, LON + 1, LAT + 2, ALT, HALF), F32)
    vmem = pl.BlockSpec(memory_space=pltpu.VMEM)
    hbm = pl.BlockSpec(memory_space=pl.ANY)
    dma = pltpu.SemaphoreType.DMA
    return pl.pallas_call(
        functools.partial(window_kernel, n_lon, n_lat),
        out_shape=(
            jax.ShapeDtypeStruct((LON, LAT, ALT, WIDE), F32),
            jax.ShapeDtypeStruct((WIDE, WIDE), BF16),
            jax.ShapeDtypeStruct((WIDE, WIDE), BF16),
        ),
        in_specs=[hbm] + [vmem] * 9,
        out_specs=(hbm, vmem, vmem),
        scratch_shapes=[
            ghosts, ghosts, ghosts, ghosts,
            pltpu.VMEM((2, LON, LAT, ALT, HALF), F32),
            pltpu.VMEM((2 * CELLS, WIDE), BF16),
            pltpu.VMEM((SEG, RAYS, HALF), F32),
            pltpu.VMEM((2 * NEAR * PAIRS, SEG, HALF), F32),
            pltpu.VMEM((2 * NEAR * RAYS, CELLS), BF16),
            pltpu.VMEM((2 * NEAR * RAYS, CELLS), BF16),
            pltpu.VMEM((STEPS, 2, 3, ROWS, HALF), F32),
            pltpu.VMEM((STEPS, 2, 2, ROWS, HALF), F32),
            pltpu.VMEM((STEPS, ROWS, HALF), F32),
            pltpu.VMEM((STEPS, ROWS, HALF), F32),
            pltpu.VMEM((WIDE, WIDE), F32),
            pltpu.VMEM((PACKED, HALF), F32),
            pltpu.VMEM((n_lat, piece, HALF), F32),
            pltpu.VMEM((piece, HALF), F32),
            pltpu.VMEM((n_lon, piece, HALF), F32),
            pltpu.VMEM((PACKED, HALF), F32),
            pltpu.VMEM((ALT, HALF), F32),
            pltpu.VMEM((2, LON, LAT, 8, HALF), F32),
            pltpu.VMEM((STEPS, ROWS, HALF), F32),
            pltpu.VMEM((STEPS, ROWS, HALF), F32),
            pltpu.VMEM((2, 8, HALF), jnp.int32),
            pltpu.VMEM((2, 8, HALF), F32),
            pltpu.VMEM((WIDE, WIDE), F32),
            pltpu.VMEM((WIDE, WIDE), F32),
            pltpu.VMEM((PANEL, WIDE), F32),
            dma, dma, dma((4,)), dma((4,)), dma((2,)), dma((2,)), dma((LON,)), dma((LON,)),
            dma((STEPS, 2)), dma((STEPS, 2)),
            dma((STEPS, 2, 2)), dma((STEPS, 2, 2)),
            dma((STEPS, 2, 2)), dma((STEPS, 2, 2)),
            dma((STEPS,)), dma((STEPS,)),
            dma((n_lat,)), dma((n_lat,)),
            dma((n_lon,)), dma((n_lon,)),
            dma((n_lat,)), dma((n_lat,)),
        ],
        compiler_params=pltpu.CompilerParams(
            collective_id=0, has_side_effects=True, vmem_limit_bytes=60 * 1024 * 1024
        ),
        cost_estimate=pl.CostEstimate(flops=12_000_000_000, bytes_accessed=6_000_000, transcendentals=0),
        name="window",
    )(*operands)


def panel_rows(block, at, *parts):
    def spread(x):
        return jnp.broadcast_to(x[:, None, :], (x.shape[0], 8, HALF))

    columns = [
        spread(jnp.broadcast_to(block[:, at + j:at + j + 1], (PANEL, HALF))[j:]) for j in range(PANEL)
    ]
    parts = [spread(part) for part in parts]
    done = [[] for _ in parts]
    for k in range(PANEL):
        scale = lax.rsqrt(columns[k][0:1])
        factor = columns[k][1:] * scale
        for n, part in enumerate(parts):
            top = part[0:1] * scale
            done[n].append(top)
            if k + 1 < PANEL:
                parts[n] = part[1:] - factor * top
        for j in range(k + 1, PANEL):
            rest = factor[j - k - 1:]
            columns[j] = columns[j] - rest * rest[0:1]
    return done


def update_matrix(packed, work, inverse, panel):
    lower = packed[0:WIDE]
    corner = lower[HALF:WIDE].T
    row = lax.broadcasted_iota(jnp.int32, (HALF, HALF), 0)
    lane = lax.broadcasted_iota(jnp.int32, (HALF, HALF), 1)
    same = (row == lane).astype(F32)
    inner = jnp.logical_and(row > 0, lane > 0)
    work[0:HALF, 0:HALF] = jnp.where(inner, lower[0:HALF], 0.0) + same
    work[0:HALF, HALF:WIDE] = jnp.where(row > 0, corner, 0.0)
    work[HALF:WIDE, 0:HALF] = jnp.where(lane > 0, lower[HALF:WIDE], 0.0)
    work[HALF:WIDE, HALF:WIDE] = packed[WIDE:PACKED] + same

    for p in range(WIDE // PANEL):
        first = p * PANEL
        side, at = first // HALF, first % HALF
        mine = slice(first, first + PANEL)
        lanes = lax.broadcasted_iota(jnp.int32, (PANEL, HALF), 1)
        rows_of = lax.broadcasted_iota(jnp.int32, (PANEL, HALF), 0)
        parts = [work[mine, 0:HALF], work[mine, HALF:WIDE]]
        block = parts[side]
        in_panel = jnp.logical_and(lanes >= at, lanes < at + PANEL)
        unit = (lanes == rows_of + at).astype(F32)
        if p == 0:
            right = jnp.logical_and(lanes == 0, rows_of > 0)
            unit = jnp.where(right, lower[mine], unit)
        parts[side] = jnp.where(in_panel, unit, block)
        for h, done in enumerate(panel_rows(block, at, *parts)):
            for i in range(PANEL):
                panel[i:i + 1, h * HALF:(h + 1) * HALF] = done[i][0, 0:1]
        done = panel[...]
        wide = lax.broadcasted_iota(jnp.int32, (PANEL, WIDE), 1)
        inverse[mine] = jnp.where(wide < first + PANEL, done, 0.0)
        rest = first + PANEL
        if rest == WIDE:
            break
        high, low = split(done)
        left = jnp.concatenate([high, high, low], axis=0)
        both = jnp.concatenate([high, low, high], axis=0)
        begin = HALF if rest >= HALF else 0
        change = lax.dot_general(
            left[:, begin:], both, (((0,), (0,)), ((), ())), preferred_element_type=F32
        )
        old = work[rest:WIDE]
        wide = lax.broadcasted_iota(jnp.int32, (WIDE - rest, WIDE), 1)
        blank = jnp.logical_and(wide >= first, wide < rest)
        if p == 0:
            start = jnp.where(lane[0:1] == 0, lower[rest:WIDE], 0.0)
            start = jnp.concatenate([start, jnp.zeros_like(start)], axis=1)
            old = jnp.where(blank, start, old)
        else:
            old = jnp.where(blank, 0.0, old)
        work[rest:WIDE] = old - change[rest - begin:]

    whole = inverse[...]
    wide = lax.broadcasted_iota(jnp.int32, (WIDE, WIDE), 1)
    tall = lax.broadcasted_iota(jnp.int32, (WIDE, WIDE), 0)
    right = jnp.where(tall[:, 0:1] > 0, whole[:, 0:1], 0.0)
    whole = jnp.where(jnp.logical_and(wide == 0, tall > 0), 0.0, whole)
    weights = jnp.sum(right * whole, axis=0, keepdims=True)
    turned = jnp.where(tall == 0, whole + weights, whole)
    return split(turned.T)


def apply_kernel(u_high, u_low, prior, end, start_out, end_out, z, results, load_sem, store_sem):
    size = CELLS // CHUNKS
    pieces = [(n, b, slice(b * size, (b + 1) * size)) for n in range(2) for b in range(CHUNKS)]
    loads = [
        pltpu.make_async_copy((prior, end)[n].at[at], z.at[n, at], load_sem.at[n, b]) for n, b, at in pieces
    ]
    stores = [
        pltpu.make_async_copy(results.at[n, at], (start_out, end_out)[n].at[at], store_sem.at[n, b])
        for n, b, at in pieces
    ]
    for copy in loads:
        copy.start()
    for (n, b, at), load, store in zip(pieces, loads, stores):
        load.wait()
        a_high, a_low = split(z[n, at])
        value = jnp.dot(jnp.concatenate([a_high, a_low], axis=0), u_high[...], preferred_element_type=F32)
        value = value[:size] + value[size:]
        value += jnp.dot(a_high, u_low[...], preferred_element_type=F32)
        results[n, at] = value
        store.start()
    for copy in stores:
        copy.wait()


def apply_update(u_high, u_low, prior, end):
    vmem = pl.BlockSpec(memory_space=pltpu.VMEM)
    hbm = pl.BlockSpec(memory_space=pl.ANY)
    out = jax.ShapeDtypeStruct((CELLS, WIDE), F32)
    return pl.pallas_call(
        apply_kernel,
        out_shape=(out, out),
        in_specs=[vmem, vmem, hbm, hbm],
        out_specs=(hbm, hbm),
        scratch_shapes=[
            pltpu.VMEM((2, CELLS, WIDE), F32),
            pltpu.VMEM((2, CELLS, WIDE), F32),
            pltpu.SemaphoreType.DMA((2, CHUNKS)),
            pltpu.SemaphoreType.DMA((2, CHUNKS)),
        ],
        compiler_params=pltpu.CompilerParams(vmem_limit_bytes=60 * 1024 * 1024),
        cost_estimate=pl.CostEstimate(flops=1_700_000_000, bytes_accessed=8_400_000, transcendentals=0),
        name="update",
    )(u_high, u_low, prior, end)


def shards(
    prior_state,
    courant,
    cell_survival_rate,
    geometry,
    entry_tile,
    entry_column,
    entry_segment,
    entry_counts,
    observed,
    obs_weight,
):
    n_lon, n_lat = lax.axis_size("lon"), lax.axis_size("lat")
    forecast, u_high, u_low = window(
        n_lon, n_lat,
        prior_state, courant.T, cell_survival_rate[None, :], geometry,
        entry_tile, entry_column, entry_segment, entry_counts, observed, obs_weight,
    )
    start_state, end_state = apply_update(
        u_high, u_low, prior_state.reshape(CELLS, WIDE), forecast.reshape(CELLS, WIDE)
    )
    return (start_state.reshape(prior_state.shape), end_state.reshape(prior_state.shape))


def solution(mesh):
    placed = (
        P("lon", "lat", None, None),
        P("lon", "lat"),
        P(),
        P(),
        P("lon", "lat", None),
        P("lon", "lat", None),
        P("lon", "lat", None),
        P("lon", "lat"),
        P(None, "lon", "lat", None),
        P(None, "lon", "lat", None),
    )
    return jax.shard_map(
        shards,
        mesh=mesh,
        in_specs=placed,
        out_specs=(P("lon", "lat", None, None), P("lon", "lat", None, None)),
        check_vma=False,
    )
```

```python
import functools
import jax
import jax.numpy as jnp
from jax import lax
from jax.experimental import pallas as pl
from jax.experimental.pallas import tpu as pltpu
from jax.sharding import PartitionSpec as P

STEPS = 4
diffusion = 0.08
highest = lax.Precision.HIGHEST
MESH = pl.DeviceIdType.MESH
F32 = jnp.float32
BF16 = jnp.bfloat16

LON, LAT, ALT, WIDE = 8, 4, 64, 256
RAYS, SEG, TILES = 128, 16, 2
ROWS = TILES * RAYS
NEAR = 3 * TILES
PAIRS = LON * LAT // 2
HALF = 128
PACKED = WIDE + HALF
PANEL = 16
CELLS = LON * LAT * ALT
CHUNKS = 4
BUILD_FIRST = 7
EARLY = 2
BESIDE_SCATTER = 3
BESIDE_ACROSS = 4
BESIDE_GATHER = 6


def split(x):
    high = x.astype(BF16)
    return high, (x - high.astype(F32)).astype(BF16)


def window_kernel(
    n_lon, n_lat,
    prior, courant, survival, geometry, entry_tile, entry_column, entry_segment, entry_counts,
    observed, obs_weight,
    end_out, u_high, u_low,
    s0, s1, s2, s3, s4, s_both, paths, counts, h_high, h_low,
    near, beside, turn_out, turn_in, gram, packed, got_lat, part, got_lon, total, decay, drifts, seen, scales,
    keys, drift_row, work, inverse, panel,
    load_sem, store_sem, swap_send, swap_recv, small_send, small_recv, back_send, back_recv,
    west_send, west_recv, row_send, row_recv, ray_send, ray_recv, turn_send, turn_recv,
    lat_send, lat_recv, lon_send, lon_recv, all_send, all_recv,
):
    lon = lax.axis_index("lon")
    lat = lax.axis_index("lat")
    group = lax.div(lat, 4)
    mine = lax.rem(lax.div(lat, 2), 2)
    core = lax.rem(lat, 2)
    theirs = 1 - mine
    partner = (lon, lat + 2 - 4 * mine)
    states = [s0, s1, s2, s3]

    def at_lon(d):
        return (lax.rem(lon + d + n_lon, n_lon), lat)

    def at_lat(d):
        return (lon, lax.rem(lat + d + n_lat, n_lat))

    def band_of(slot):
        return 4 * group + 2 * slot + core

    def holder(band):
        to = (lon, 4 * lax.div(band, 4) + 2 * mine + lax.rem(band, 2))
        return to, lax.rem(lax.div(band, 2), 2)

    def has_up(slot):
        return band_of(slot) + 1 < n_lat

    def has_down(slot):
        return band_of(slot) > 0

    def remote(src, dst, send, recv, to):
        return pltpu.make_async_remote_copy(
            src_ref=src, dst_ref=dst, send_sem=send, recv_sem=recv, device_id=to, device_id_type=MESH
        )

    def half(index):
        return pl.ds(pl.multiple_of(index * HALF, HALF), HALF)

    cells_of = (slice(1, LON + 1), slice(1, LAT + 1))
    loads = pltpu.make_async_copy(prior.at[:, :, :, half(mine)], s0.at[(mine,) + cells_of], load_sem)
    loads.start()

    slots = entry_tile.shape[2]
    column = entry_column[0]
    live = lax.broadcasted_iota(jnp.int32, (1, slots), 1) < entry_counts[...]
    near_key = (entry_tile[0] - (lat - 1) * TILES) * PAIRS + column // 2
    near_key = jnp.where(live, near_key, -1)
    path_key = entry_segment[0] * 2 + column % 2
    keys[0, 0:1, 0:slots] = near_key
    keys[0, 1:2, 0:slots] = path_key
    drift_row[0, 0:LAT, 0:LON] = courant[...]

    barrier = pltpu.get_barrier_semaphore()
    for d in range(1, n_lon):
        pl.semaphore_signal(barrier, inc=1, device_id=at_lon(d), device_id_type=MESH)
    for d in range(1, n_lat):
        pl.semaphore_signal(barrier, inc=1, device_id=at_lat(d), device_id_type=MESH)
    pl.semaphore_wait(barrier, n_lon + n_lat - 2)

    swaps = ((0, LON, 0, 1), (0, LON, LAT - 1, LAT), (LON - 1, LON, 1, LAT - 1), (0, LON - 1, 1, LAT - 1))

    def swap(n, slot):
        i, i_end, j, j_end = swaps[n]
        return remote(
            prior.at[i:i_end, j:j_end, :, half(theirs)],
            s0.at[slot, i + 1:i_end + 1, j + 1:j_end + 1],
            swap_send.at[n], swap_recv.at[n], partner,
        )

    small = [
        remote(keys.at[0], keys.at[1], small_send.at[0], small_recv.at[0], partner),
        remote(drift_row.at[0], drift_row.at[1], small_send.at[1], small_recv.at[1], partner),
    ]
    for copy in small:
        copy.start()
    for n in range(len(swaps)):
        swap(n, mine).start()

    def back(i):
        return remote(
            s4.at[theirs, i], end_out.at[i, :, :, half(mine)], back_send.at[i], back_recv.at[i], partner
        )

    def back_landed(i):
        return remote(
            s4.at[theirs, i], end_out.at[i, :, :, half(theirs)], back_send.at[i], back_recv.at[i], partner
        )

    def west_copy(k, s):
        state = states[k]
        return remote(
            state.at[s, LON, 1:LAT + 1], state.at[s, 0, 1:LAT + 1],
            west_send.at[k, s], west_recv.at[k, s], at_lon(1),
        )

    def row_copy(k, s, up):
        to, slot = holder(band_of(s) + (1 if up else -1))
        state = states[k]
        src = state.at[s, 1:LON + 1, LAT if up else 1]
        dst = state.at[slot, 1:LON + 1, 0 if up else LAT + 1]
        return remote(src, dst, row_send.at[k, s, up], row_recv.at[k, slot, up], to)

    def row_landed(k, s, up):
        state = states[k]
        ref = state.at[s, 1:LON + 1, 0 if up else LAT + 1]
        return remote(ref, ref, row_send.at[k, s, up], row_recv.at[k, s, up], partner)

    def ray_copy(k, s, up):
        to, slot = holder(band_of(s) + (1 if up else -1))
        return remote(
            near.at[k, s, 2 if up else 0], beside.at[k, slot, up],
            ray_send.at[k, s, up], ray_recv.at[k, slot, up], to,
        )

    def ray_landed(k, s, up):
        ref = beside.at[k, s, up]
        return remote(ref, ref, ray_send.at[k, s, up], ray_recv.at[k, s, up], partner)

    def turn_copy(k):
        return remote(turn_out.at[k], turn_in.at[k], turn_send.at[k], turn_recv.at[k], partner)

    def out_both(make, k, s, act):
        @pl.when(has_up(s))
        def _():
            act(make(k, s, 1))

        @pl.when(has_down(s))
        def _():
            act(make(k, s, 0))

    def in_both(make, k, s):
        @pl.when(has_down(s))
        def _():
            make(k, s, 1).wait_recv()

        @pl.when(has_up(s))
        def _():
            make(k, s, 0).wait_recv()

    def begin(copy):
        copy.start()

    def sent(copy):
        copy.wait_send()

    def send_edges(k, s):
        out_both(row_copy, k, s, begin)
        west_copy(k, s).start()

    loads.wait()
    send_edges(0, mine)

    for s, up, row, missing in ((0, 1, 0, has_down(0)), (1, 0, LAT + 1, has_up(1))):
        @pl.when(jnp.logical_not(missing))
        def _(s=s, up=up, row=row):
            for k in range(STEPS):
                def clear(i, c, k=k):
                    states[k][s, i + 1, row] = jnp.zeros((ALT, HALF), F32)
                    return c
                lax.fori_loop(0, LON, clear, 0)
                beside[k, s, up] = jnp.zeros((ROWS, HALF), F32)

    def upright(line):
        return jnp.broadcast_to(line, (HALF, HALF)).T

    line = survival[...]
    decay[...] = upright(jnp.concatenate([line, line], axis=1))[0:ALT]
    for k in range(STEPS):
        for t in range(TILES):
            seen[k, t * RAYS:(t + 1) * RAYS] = upright(observed[k, 0, t:t + 1])
            scales[k, t * RAYS:(t + 1) * RAYS] = upright(obs_weight[k, 0, t:t + 1])

    def turn_path(s, c):
        block = geometry[s]
        paths[s] = jnp.concatenate([block, block], axis=0).T
        return c

    lax.fori_loop(0, SEG, turn_path, 0)

    for copy in small:
        copy.wait_recv()
    wide_half = lax.broadcasted_iota(jnp.int32, (HALF, slots), 0) // ALT
    for slot in range(2):
        own = mine == slot
        at_key = jnp.where(own, keys[0, 0:1, 0:slots], keys[1, 0:1, 0:slots])
        by_path = jnp.where(own, keys[0, 1:2, 0:slots], keys[1, 1:2, 0:slots])
        left = (lax.broadcasted_iota(jnp.int32, (NEAR * PAIRS, slots), 0) == at_key).astype(F32).astype(BF16)
        for s in range(SEG):
            right = (wide_half + 2 * s == by_path).astype(F32).astype(BF16)
            counts[slot * NEAR * PAIRS:(slot + 1) * NEAR * PAIRS, s] = lax.dot_general(
                left, right, (((1,), (1,)), ((), ())), preferred_element_type=F32
            )
        drift_of = jnp.where(own, drift_row[0], drift_row[1])
        for i in range(LON):
            across_lanes = jnp.broadcast_to(drift_of[:, i:i + 1], (8, HALF))
            for j in range(LAT):
                drifts[slot, i, j] = jnp.broadcast_to(across_lanes[j:j + 1], (8, HALF))

    def build_tile(t, c):
        def build(p, c2):
            number = counts[t * PAIRS + p]
            total_path = number[0:1] * paths[0]
            for s in range(1, SEG):
                total_path += number[s:s + 1] * paths[s]
            high, low = split(total_path)
            at = (pl.ds(pl.multiple_of(t * RAYS, RAYS), RAYS), half(p))
            h_high[at] = high
            h_low[at] = low
            return c2

        return lax.fori_loop(0, PAIRS, build, c)

    lax.fori_loop(0, BUILD_FIRST, build_tile, 0)
    for n in range(3):
        swap(n, theirs).wait_recv()
    send_edges(0, theirs)
    lax.fori_loop(BUILD_FIRST, 2 * NEAR, build_tile, 0)
    gram[...] = jnp.zeros((WIDE, WIDE), F32)

    def cell(k, s, i, j):
        old = states[k]
        drift = drifts[s, i, j, 0:1]
        keep = 1.0 - 2.0 * diffusion - drift
        new = keep * old[s, i + 1, j + 1] + drift * old[s, i, j + 1]
        new += diffusion * (old[s, i + 1, j + 2] + old[s, i + 1, j])
        new = new * decay[...]
        if k + 1 < STEPS:
            states[k + 1][s, i + 1, j + 1] = new
        else:
            s4[s, i, j] = new
        at = pl.ds(pl.multiple_of(s * CELLS, CELLS) + (i * LAT + j) * ALT, ALT)
        high, low = split(new)
        s_both[at, 0:HALF] = high
        s_both[at, HALF:WIDE] = low

    def one_slot(k, s, first, last, rows):
        for i in range(first, last):
            for j in rows:
                cell(k, s, i, j)

    def cells(k, first, last, rows):
        def one(s, c):
            one_slot(k, s, first, last, rows)
            return c

        lax.fori_loop(0, 2, one, 0)

    def project(k):
        for s, begin_at, step, number in ((0, 0, 2, 2), (1, 0, 2, 2), (0, 1, 0, 1), (1, 1, 0, 1)):
            def part_of(n, c, s=s, begin_at=begin_at, step=step):
                t = begin_at + step * n
                first = s * NEAR * RAYS + t * ROWS
                rays = pl.ds(pl.multiple_of(first, ROWS), ROWS)
                add = jnp.dot(h_high[rays], s_both[s * CELLS:(s + 1) * CELLS], preferred_element_type=F32)
                add = add[:, 0:HALF] + add[:, HALF:WIDE]
                add += jnp.dot(
                    h_low[rays], s_both[s * CELLS:(s + 1) * CELLS, 0:HALF], preferred_element_type=F32
                )
                near[k, s, t] = add
                return c

            lax.fori_loop(0, number, part_of, 0)
            if step:
                out_both(ray_copy, k, s, begin)

    def turn(k):
        in_both(ray_landed, k, theirs)
        turn_out[k] = near[k, theirs, 1] + beside[k, theirs, 0] + beside[k, theirs, 1]
        turn_copy(k).start()

    def add_gram(k):
        in_both(ray_landed, k, mine)
        here = near[k, mine, 1] + beside[k, mine, 0] + beside[k, mine, 1]
        turn_copy(k).wait_recv()
        there = turn_in[k]
        first = mine == 0
        low = jnp.where(first, here, there)
        high = jnp.where(first, there, here)
        lane = lax.broadcasted_iota(jnp.int32, (ROWS, HALF), 1)
        low = jnp.where(lane == 0, seen[k] - low, low) * scales[k]
        high = high * scales[k]
        rays = jnp.concatenate([low, high], axis=1)
        high, low = split(rays)
        left_high, left_low = split(rays.T)
        gram[...] += jnp.dot(
            jnp.concatenate([left_high, left_high, left_low], axis=1),
            jnp.concatenate([high, low, high], axis=0),
            preferred_element_type=F32,
        )

    one_slot(0, mine, 1, LON, range(1, LAT - 1))
    swap(3, theirs).wait_recv()
    one_slot(0, theirs, 1, LON, range(1, LAT - 1))
    for k in range(STEPS):
        if k > 0:
            cells(k, 1, LON, range(1, LAT - 1))
        for s in range(2):
            west_copy(k, s).wait_recv()
        cells(k, 0, 1, range(1, LAT - 1))
        for s in range(2):
            in_both(row_landed, k, s)
        cells(k, 0, LON, (0, LAT - 1))
        if k + 1 < STEPS:
            for s in range(2):
                send_edges(k + 1, s)
        else:
            store = pltpu.make_async_copy(s4.at[mine], end_out.at[:, :, :, half(mine)], store_sem)
            store.start()
            for i in range(EARLY):
                back(i).start()
        if k > 0:
            turn(k - 1)
        project(k)
        if 1 < k < STEPS - 1:
            add_gram(k - 2)
    turn(STEPS - 1)
    for k in range(STEPS - 3, STEPS):
        add_gram(k)

    packed[0:WIDE] = gram[:, 0:HALF]
    packed[WIDE:PACKED] = gram[HALF:WIDE, HALF:WIDE]
    piece = PACKED // n_lat

    def own(index):
        return pl.ds(pl.multiple_of(index * piece, 8), piece)

    def scatter(d):
        to = lax.rem(lat + d, n_lat)
        return remote(packed.at[own(to)], got_lat.at[d], lat_send.at[d], lat_recv.at[d], at_lat(d))

    def across(d):
        return remote(part, got_lon.at[d], lon_send.at[d], lon_recv.at[d], at_lon(d))

    def gather(d):
        return remote(total.at[own(lat)], total.at[own(lat)], all_send.at[d], all_recv.at[d], at_lat(d))

    def landed(d):
        from_lat = lax.rem(lat - d + n_lat, n_lat)
        return remote(total.at[own(from_lat)], total.at[own(from_lat)], all_send.at[d], all_recv.at[d], at_lat(d))

    for d in range(1, n_lat):
        scatter(d).start()
    for i in range(EARLY, BESIDE_SCATTER):
        back(i).start()
    acc = packed[own(lat)]
    for d in range(1, n_lat):
        scatter(d).wait_recv()
        acc += got_lat[d]
    part[...] = acc
    for d in range(1, n_lon):
        across(d).start()
    for i in range(BESIDE_SCATTER, BESIDE_ACROSS):
        back(i).start()
    for d in range(1, n_lon):
        across(d).wait_recv()
        acc += got_lon[d]
    total[own(lat)] = acc
    for d in range(1, n_lat):
        gather(d).start()
    for i in range(BESIDE_ACROSS, BESIDE_GATHER):
        back(i).start()
    for d in range(1, n_lat):
        landed(d).wait_recv()
    for i in range(BESIDE_GATHER, LON):
        back(i).start()
    u_high[...], u_low[...] = update_matrix(total, work, inverse, panel)

    store.wait()
    for i in range(LON):
        back_landed(i).wait_recv()
        back(i).wait_send()
    for n in range(len(swaps)):
        swap(n, mine).wait_send()
    for copy in small:
        copy.wait_send()
    for k in range(STEPS):
        turn_copy(k).wait_send()
        for s in range(2):
            west_copy(k, s).wait_send()
            out_both(row_copy, k, s, sent)
            out_both(ray_copy, k, s, sent)
    for d in range(1, n_lat):
        scatter(d).wait_send()
        gather(d).wait_send()
    for d in range(1, n_lon):
        across(d).wait_send()


def window(n_lon, n_lat, *operands):
    piece = PACKED // n_lat
    ghosts = pltpu.VMEM((2, LON + 1, LAT + 2, ALT, HALF), F32)
    vmem = pl.BlockSpec(memory_space=pltpu.VMEM)
    hbm = pl.BlockSpec(memory_space=pl.ANY)
    dma = pltpu.SemaphoreType.DMA
    return pl.pallas_call(
        functools.partial(window_kernel, n_lon, n_lat),
        out_shape=(
            jax.ShapeDtypeStruct((LON, LAT, ALT, WIDE), F32),
            jax.ShapeDtypeStruct((WIDE, WIDE), BF16),
            jax.ShapeDtypeStruct((WIDE, WIDE), BF16),
        ),
        in_specs=[hbm] + [vmem] * 9,
        out_specs=(hbm, vmem, vmem),
        scratch_shapes=[
            ghosts, ghosts, ghosts, ghosts,
            pltpu.VMEM((2, LON, LAT, ALT, HALF), F32),
            pltpu.VMEM((2 * CELLS, WIDE), BF16),
            pltpu.VMEM((SEG, RAYS, HALF), F32),
            pltpu.VMEM((2 * NEAR * PAIRS, SEG, HALF), F32),
            pltpu.VMEM((2 * NEAR * RAYS, CELLS), BF16),
            pltpu.VMEM((2 * NEAR * RAYS, CELLS), BF16),
            pltpu.VMEM((STEPS, 2, 3, ROWS, HALF), F32),
            pltpu.VMEM((STEPS, 2, 2, ROWS, HALF), F32),
            pltpu.VMEM((STEPS, ROWS, HALF), F32),
            pltpu.VMEM((STEPS, ROWS, HALF), F32),
            pltpu.VMEM((WIDE, WIDE), F32),
            pltpu.VMEM((PACKED, HALF), F32),
            pltpu.VMEM((n_lat, piece, HALF), F32),
            pltpu.VMEM((piece, HALF), F32),
            pltpu.VMEM((n_lon, piece, HALF), F32),
            pltpu.VMEM((PACKED, HALF), F32),
            pltpu.VMEM((ALT, HALF), F32),
            pltpu.VMEM((2, LON, LAT, 8, HALF), F32),
            pltpu.VMEM((STEPS, ROWS, HALF), F32),
            pltpu.VMEM((STEPS, ROWS, HALF), F32),
            pltpu.VMEM((2, 8, HALF), jnp.int32),
            pltpu.VMEM((2, 8, HALF), F32),
            pltpu.VMEM((WIDE, WIDE), F32),
            pltpu.VMEM((WIDE, WIDE), F32),
            pltpu.VMEM((PANEL, WIDE), F32),
            dma, dma, dma((4,)), dma((4,)), dma((2,)), dma((2,)), dma((LON,)), dma((LON,)),
            dma((STEPS, 2)), dma((STEPS, 2)),
            dma((STEPS, 2, 2)), dma((STEPS, 2, 2)),
            dma((STEPS, 2, 2)), dma((STEPS, 2, 2)),
            dma((STEPS,)), dma((STEPS,)),
            dma((n_lat,)), dma((n_lat,)),
            dma((n_lon,)), dma((n_lon,)),
            dma((n_lat,)), dma((n_lat,)),
        ],
        compiler_params=pltpu.CompilerParams(
            collective_id=0, has_side_effects=True, vmem_limit_bytes=60 * 1024 * 1024
        ),
        cost_estimate=pl.CostEstimate(flops=12_000_000_000, bytes_accessed=6_000_000, transcendentals=0),
        name="window",
    )(*operands)


def panel_rows(block, at, *parts):
    def spread(x):
        return jnp.broadcast_to(x[:, None, :], (x.shape[0], 8, HALF))

    columns = [
        spread(jnp.broadcast_to(block[:, at + j:at + j + 1], (PANEL, HALF))[j:]) for j in range(PANEL)
    ]
    parts = [spread(part) for part in parts]
    done = [[] for _ in parts]
    for k in range(PANEL):
        scale = lax.rsqrt(columns[k][0:1])
        factor = columns[k][1:] * scale
        for n, part in enumerate(parts):
            top = part[0:1] * scale
            done[n].append(top)
            if k + 1 < PANEL:
                parts[n] = part[1:] - factor * top
        for j in range(k + 1, PANEL):
            rest = factor[j - k - 1:]
            columns[j] = columns[j] - rest * rest[0:1]
    return done


def update_matrix(packed, work, inverse, panel):
    lower = packed[0:WIDE]
    corner = lower[HALF:WIDE].T
    row = lax.broadcasted_iota(jnp.int32, (HALF, HALF), 0)
    lane = lax.broadcasted_iota(jnp.int32, (HALF, HALF), 1)
    same = (row == lane).astype(F32)
    inner = jnp.logical_and(row > 0, lane > 0)
    work[0:HALF, 0:HALF] = jnp.where(inner, lower[0:HALF], 0.0) + same
    work[0:HALF, HALF:WIDE] = jnp.where(row > 0, corner, 0.0)
    work[HALF:WIDE, 0:HALF] = jnp.where(lane > 0, lower[HALF:WIDE], 0.0)
    work[HALF:WIDE, HALF:WIDE] = packed[WIDE:PACKED] + same

    for p in range(WIDE // PANEL):
        first = p * PANEL
        side, at = first // HALF, first % HALF
        mine = slice(first, first + PANEL)
        lanes = lax.broadcasted_iota(jnp.int32, (PANEL, HALF), 1)
        rows_of = lax.broadcasted_iota(jnp.int32, (PANEL, HALF), 0)
        parts = [work[mine, 0:HALF], work[mine, HALF:WIDE]]
        block = parts[side]
        in_panel = jnp.logical_and(lanes >= at, lanes < at + PANEL)
        unit = (lanes == rows_of + at).astype(F32)
        if p == 0:
            right = jnp.logical_and(lanes == 0, rows_of > 0)
            unit = jnp.where(right, lower[mine], unit)
        parts[side] = jnp.where(in_panel, unit, block)
        for h, done in enumerate(panel_rows(block, at, *parts)):
            for i in range(PANEL):
                panel[i:i + 1, h * HALF:(h + 1) * HALF] = done[i][0, 0:1]
        done = panel[...]
        wide = lax.broadcasted_iota(jnp.int32, (PANEL, WIDE), 1)
        inverse[mine] = jnp.where(wide < first + PANEL, done, 0.0)
        rest = first + PANEL
        if rest == WIDE:
            break
        high, low = split(done)
        left = jnp.concatenate([high, high, low], axis=0)
        both = jnp.concatenate([high, low, high], axis=0)
        begin = HALF if rest >= HALF else 0
        change = lax.dot_general(
            left[:, begin:], both, (((0,), (0,)), ((), ())), preferred_element_type=F32
        )
        old = work[rest:WIDE]
        wide = lax.broadcasted_iota(jnp.int32, (WIDE - rest, WIDE), 1)
        blank = jnp.logical_and(wide >= first, wide < rest)
        if p == 0:
            start = jnp.where(lane[0:1] == 0, lower[rest:WIDE], 0.0)
            start = jnp.concatenate([start, jnp.zeros_like(start)], axis=1)
            old = jnp.where(blank, start, old)
        else:
            old = jnp.where(blank, 0.0, old)
        work[rest:WIDE] = old - change[rest - begin:]

    whole = inverse[...]
    wide = lax.broadcasted_iota(jnp.int32, (WIDE, WIDE), 1)
    tall = lax.broadcasted_iota(jnp.int32, (WIDE, WIDE), 0)
    right = jnp.where(tall[:, 0:1] > 0, whole[:, 0:1], 0.0)
    whole = jnp.where(jnp.logical_and(wide == 0, tall > 0), 0.0, whole)
    weights = jnp.sum(right * whole, axis=0, keepdims=True)
    turned = jnp.where(tall == 0, whole + weights, whole)
    return split(turned.T)


def apply_kernel(u_high, u_low, prior, end, start_out, end_out, z, results, load_sem, store_sem):
    size = CELLS // CHUNKS
    pieces = [(n, b, slice(b * size, (b + 1) * size)) for n in range(2) for b in range(CHUNKS)]
    loads = [
        pltpu.make_async_copy((prior, end)[n].at[at], z.at[n, at], load_sem.at[n, b]) for n, b, at in pieces
    ]
    stores = [
        pltpu.make_async_copy(results.at[n, at], (start_out, end_out)[n].at[at], store_sem.at[n, b])
        for n, b, at in pieces
    ]
    for copy in loads:
        copy.start()
    for (n, b, at), load, store in zip(pieces, loads, stores):
        load.wait()
        a_high, a_low = split(z[n, at])
        value = jnp.dot(jnp.concatenate([a_high, a_low], axis=0), u_high[...], preferred_element_type=F32)
        value = value[:size] + value[size:]
        value += jnp.dot(a_high, u_low[...], preferred_element_type=F32)
        results[n, at] = value
        store.start()
    for copy in stores:
        copy.wait()


def apply_update(u_high, u_low, prior, end):
    vmem = pl.BlockSpec(memory_space=pltpu.VMEM)
    hbm = pl.BlockSpec(memory_space=pl.ANY)
    out = jax.ShapeDtypeStruct((CELLS, WIDE), F32)
    return pl.pallas_call(
        apply_kernel,
        out_shape=(out, out),
        in_specs=[vmem, vmem, hbm, hbm],
        out_specs=(hbm, hbm),
        scratch_shapes=[
            pltpu.VMEM((2, CELLS, WIDE), F32),
            pltpu.VMEM((2, CELLS, WIDE), F32),
            pltpu.SemaphoreType.DMA((2, CHUNKS)),
            pltpu.SemaphoreType.DMA((2, CHUNKS)),
        ],
        compiler_params=pltpu.CompilerParams(vmem_limit_bytes=60 * 1024 * 1024),
        cost_estimate=pl.CostEstimate(flops=1_700_000_000, bytes_accessed=8_400_000, transcendentals=0),
        name="update",
    )(u_high, u_low, prior, end)


def shards(
    prior_state,
    courant,
    cell_survival_rate,
    geometry,
    entry_tile,
    entry_column,
    entry_segment,
    entry_counts,
    observed,
    obs_weight,
):
    n_lon, n_lat = lax.axis_size("lon"), lax.axis_size("lat")
    forecast, u_high, u_low = window(
        n_lon, n_lat,
        prior_state, courant.T, cell_survival_rate[None, :], geometry,
        entry_tile, entry_column, entry_segment, entry_counts, observed, obs_weight,
    )
    start_state, end_state = apply_update(
        u_high, u_low, prior_state.reshape(CELLS, WIDE), forecast.reshape(CELLS, WIDE)
    )
    return (start_state.reshape(prior_state.shape), end_state.reshape(prior_state.shape))


def solution(mesh):
    placed = (
        P("lon", "lat", None, None),
        P("lon", "lat"),
        P(),
        P(),
        P("lon", "lat", None),
        P("lon", "lat", None),
        P("lon", "lat", None),
        P("lon", "lat"),
        P(None, "lon", "lat", None),
        P(None, "lon", "lat", None),
    )
    return jax.shard_map(
        shards,
        mesh=mesh,
        in_specs=placed,
        out_specs=(P("lon", "lat", None, None), P("lon", "lat", None, None)),
        check_vma=False,
    )
```
